256 devices in a mesh: ctx: 64 (over x, z_lo, y), fsdp: 4 (over z_hi, core).
Axes of the slice: x: 4, y: 4, z: 8 (z_hi: 2, z_lo: 4; z = z_hi * 4 + z_lo), core: 2. Of those that a mesh axis runs over, the one named last changes fastest.
Arguments:
- inputs: bfloat16 [4, 16384, 4096], P('fsdp', 'ctx'), may hold values from -6 to 6
- gates: bfloat16 [4, 16384, 4096], P('fsdp', 'ctx'), may hold values from -6 to 6
- grad_out: bfloat16 [4, 16384, 4096], P('fsdp', 'ctx'), may hold values from -6 to 6
- doc_lengths: int32 [4, 64], P('fsdp'), may hold values from 1 to 1024, 16384 in all within a row
- short_filter: bfloat16 [7, 256], P(None, 'fsdp'), may hold values from -2 to 2
- long_filter: bfloat16 [128, 256], P(None, 'fsdp'), may hold values from -0.5 to 0.5
Outputs:
- grad_inputs: bfloat16 [4, 16384, 4096], P('fsdp', 'ctx')
- grad_gates: bfloat16 [4, 16384, 4096], P('fsdp', 'ctx')
- short_grad: float32 [7, 256], P(None, 'fsdp')
- long_grad: float32 [128, 256], P(None, 'fsdp')
The draws below stay inside these ranges and needn't reach their ends.
Inputs may be any that keep to these rules, and one draw needn't show every extreme that they name: `doc_lengths`: each pack's 64 lengths sum to 16384, and one of them is exactly 1024.
All inputs are finite; a program needn't handle non-finite values.
Results may differ from the reference program's by a relative error of at most 0.012.
Values may be sent and summed in bfloat16 or wider, within the bound.
A program may use at most 128 MiB of HBM per device.

```python
import math
import jax
import jax.numpy as jnp
import numpy as np
from jax import lax

CH = 4096
SE_TAPS = 7
MR_TAPS = 128
GROUPS = 256
SEQ = 16384
PACKS = 4
DOCS = 64
DOC_MOST = 1024


def level_of(own_key, shape, split, smallest, top_value):
    loudness = 1.0
    for axis_at, parts in split:
        steps = jax.random.uniform(jax.random.fold_in(jax.random.fold_in(own_key, 6), axis_at), (parts,), jnp.float32, smallest / len(split), top_value / len(split))
        loudness = loudness * jnp.repeat(jnp.exp(steps), shape[axis_at] // parts).reshape((-1,) + (1,) * (len(shape) - 1 - axis_at))
    return loudness


def split_up(number_of, total, reach, skew):
    portions = [(1 << 20) // math.isqrt(grade ** skew) + 1 for grade in range(2, number_of + 1)]
    surplus, holding = total - reach - (number_of - 1), [1] * (number_of - 1)
    while surplus > 0:
        free = [i for i in range(number_of - 1) if holding[i] < reach]
        pool, remaining = sum([portions[i] for i in free]), surplus
        for i in free:
            more = min(reach - holding[i], max(1, remaining * portions[i] // pool), surplus)
            holding[i] = holding[i] + more
            surplus = surplus - more
    return np.array([reach] + holding)


def ragged(rng, amount, total, bound, lean):
    if amount == 2:
        one = jax.random.randint(rng, (), max(1, total - bound), min(bound, total - 1) + 1)
        return jnp.stack([one, total - one])
    sizes = jnp.asarray(split_up(amount, total, bound, lean), jnp.int32)
    pairs = (amount - 1) // 2
    donor, sink = sizes[1:1 + 2 * pairs:2], sizes[2:2 + 2 * pairs:2]
    room = jnp.minimum(donor - 1, bound - sink)
    moved = jax.random.randint(jax.random.fold_in(rng, 1), (pairs,), 0, 1 << 20) % (room + 1)
    sizes = sizes.at[1:1 + 2 * pairs:2].set(donor - moved).at[2:2 + 2 * pairs:2].set(sink + moved)
    return sizes[jax.random.permutation(jax.random.fold_in(rng, 2), amount)]


def noise(rng, extent, scale, limit, shards=(), held_as=jnp.bfloat16):
    result = scale * jax.random.normal(rng, extent, jnp.float32)
    if shards:
        result = result * level_of(rng, extent, shards, -0.22, 0.18)
    return jnp.clip(result, -limit, limit).astype(held_as)


def setup_inputs(seed: int = 0) -> dict:
    keys = jax.random.split(jax.random.key(seed), 7)
    inputs = noise(keys[0], (PACKS, SEQ, CH), 1.0, 6.0, ((0, 4), (1, 64)))
    gates = noise(keys[1], (PACKS, SEQ, CH), 1.0, 6.0, ((0, 4), (1, 64)))
    grad_out = noise(keys[2], (PACKS, SEQ, CH), 1.0, 6.0, ((0, 4), (1, 64)))
    doc_lengths = jax.vmap(lambda own: ragged(own, DOCS, SEQ, DOC_MOST, 2))(jax.random.split(keys[3], PACKS)).reshape((PACKS, DOCS)).astype(jnp.int32)
    short_filter = noise(keys[4], (SE_TAPS, GROUPS), SE_TAPS ** -0.5, 2.0, ((1, 4),))
    long_filter = noise(keys[5], (MR_TAPS, GROUPS), MR_TAPS ** -0.5, 0.5, ((1, 4),))
    return {"inputs": inputs, "gates": gates, "grad_out": grad_out, "doc_lengths": doc_lengths, "short_filter": short_filter, "long_filter": long_filter}


def doc_starts(lengths, positions):
    doc_ends = jnp.cumsum(lengths).astype(jnp.int32)
    passed = (doc_ends[None, :] <= positions[:, None]).astype(jnp.int32)
    return lax.optimization_barrier(jnp.sum(passed * lengths[None, :], axis=1)).astype(jnp.int32)

def block_mask(lengths, source_pos, target_pos):
    return source_pos[:, None] >= doc_starts(lengths, target_pos)[None, :]

def channel_table(filters, channels):
    tap_count, groups = filters.shape
    spread = jnp.broadcast_to(filters[:, :, None], (tap_count, groups, channels // groups))
    return spread.reshape(tap_count, channels).astype(jnp.float32)

def band_matrix(filters):
    tap_count, groups = filters.shape
    repeated = jnp.broadcast_to(jnp.transpose(filters)[:, None, :], (groups, tap_count, tap_count))
    padded = jnp.pad(repeated, ((0, 0), (0, 0), (0, tap_count + 1)))
    flattened = padded.reshape(groups, tap_count * (2 * tap_count + 1))[:, :2 * tap_count * tap_count]
    return flattened.reshape(groups, tap_count, 2 * tap_count)

def diagonal_sums(correlation):
    groups, tap_count, span_rows = correlation.shape
    flattened = jnp.pad(correlation.reshape(groups, tap_count * span_rows), ((0, 0), (0, tap_count)))
    skewed = flattened.reshape(groups, tap_count, span_rows + 1)[:, :, :tap_count]
    return jnp.transpose(lax.optimization_barrier(jnp.sum(skewed, axis=1)))

def short_forward(padded_rows, channel_taps, positions, starts):
    tap_count = channel_taps.shape[0]
    row_count = padded_rows.shape[0] - (tap_count - 1)
    accumulated = jnp.zeros((row_count, padded_rows.shape[1]), jnp.float32)
    for offset in range(tap_count):
        shifted = padded_rows[tap_count - 1 - offset:tap_count - 1 - offset + row_count]
        in_doc = (positions - offset >= starts).astype(jnp.float32)[:, None]
        accumulated = accumulated + in_doc * channel_taps[offset][None, :] * shifted.astype(jnp.float32)
    return accumulated

def short_backward(act_ext, inputs_rows, channel_taps, positions, ext_starts, groups):
    tap_count = channel_taps.shape[0]
    row_count, channels = inputs_rows.shape
    accumulated = jnp.zeros((row_count, channels), jnp.float32)
    tap_terms = []
    for offset in range(tap_count):
        shifted = act_ext[offset:offset + row_count].astype(jnp.float32)
        in_doc = (positions >= ext_starts[offset:offset + row_count]).astype(jnp.float32)[:, None]
        masked = in_doc * shifted
        accumulated = accumulated + channel_taps[offset][None, :] * masked
        product = masked * inputs_rows.astype(jnp.float32)
        tap_terms.append(lax.optimization_barrier(jnp.sum(product.reshape(row_count, groups, channels // groups), axis=(0, 2))))
    return (accumulated, jnp.stack(tap_terms))

def long_terms(band_table, cot_ext, gated_rows, lengths):
    groups, tap_count, span_rows = band_table.shape
    row_count, channels = gated_rows.shape
    group_width = channels // groups

    def one_block(block_index):
        block_start = block_index * tap_count
        window = lax.dynamic_slice_in_dim(cot_ext, block_start, span_rows, 0).astype(jnp.float32)
        own_rows = lax.dynamic_slice_in_dim(gated_rows, block_start, tap_count, 0).astype(jnp.float32)
        source_pos = block_start + lax.iota(jnp.int32, tap_count)
        target_pos = block_start + lax.iota(jnp.int32, span_rows)
        in_document = block_mask(lengths, source_pos, target_pos).astype(jnp.float32)
        kernel = band_table.astype(jnp.float32) * in_document[None]
        stacked = window.reshape(span_rows, groups, group_width)
        back_grad = jnp.einsum('gst,tgc->sgc', kernel, stacked).reshape(tap_count, channels)
        correlation = jnp.einsum('sgc,tgc->gst', own_rows.reshape(tap_count, groups, group_width), stacked)
        correlation = correlation * in_document[None]
        return (back_grad, diagonal_sums(correlation))
    back_blocks, tap_blocks = lax.map(one_block, jnp.arange(row_count // tap_count, dtype=jnp.int32))
    return (back_blocks.reshape(row_count, channels), lax.optimization_barrier(jnp.sum(tap_blocks, axis=0)))

def reference(inputs, gates, grad_out, doc_lengths, short_filter, long_filter):
    pack_count, seq_rows, channels = inputs.shape
    short_count, groups = short_filter.shape
    long_count = long_filter.shape[0]
    short_reach = short_count - 1
    channel_taps = channel_table(short_filter, channels)
    band_table = band_matrix(long_filter)
    positions = lax.iota(jnp.int32, seq_rows)
    ext_positions = lax.iota(jnp.int32, seq_rows + short_reach)
    grads_in = []
    grads_gate = []
    short_total = jnp.zeros((short_count, groups), jnp.float32)
    long_total = jnp.zeros((long_count, groups), jnp.float32)
    for pack_index in range(pack_count):
        inputs_rows = inputs[pack_index]
        gate_values = gates[pack_index].astype(jnp.float32)
        cotangent = grad_out[pack_index]
        lengths = doc_lengths[pack_index]
        starts = doc_starts(lengths, positions)
        padded_rows = jnp.concatenate([jnp.zeros((short_reach, channels), inputs.dtype), inputs_rows], axis=0)
        activation = short_forward(padded_rows, channel_taps, positions, starts).astype(jnp.bfloat16)
        gated_rows = (gate_values * activation.astype(jnp.float32)).astype(jnp.bfloat16)
        cot_ext = jnp.concatenate([cotangent, jnp.zeros((long_count, channels), grad_out.dtype)], axis=0)
        back_grad, long_part = long_terms(band_table, cot_ext, gated_rows, lengths)
        act_grad = (back_grad * gate_values).astype(jnp.bfloat16)
        grads_gate.append((back_grad * activation.astype(jnp.float32)).astype(jnp.bfloat16))
        act_ext = jnp.concatenate([act_grad, jnp.zeros((short_reach, channels), act_grad.dtype)], axis=0)
        ext_starts = doc_starts(lengths, ext_positions)
        grad_in, short_part = short_backward(act_ext, inputs_rows, channel_taps, positions, ext_starts, groups)
        grads_in.append(grad_in.astype(jnp.bfloat16))
        short_total = short_total + short_part
        long_total = long_total + long_part
    normalizer = 1.0 / math.sqrt(pack_count * seq_rows)
    return (jnp.stack(grads_in), jnp.stack(grads_gate), short_total * normalizer, long_total * normalizer)
```

```python
import functools
import math

import jax
import jax.numpy as jnp
from jax import lax
from jax.experimental import pallas as pl
from jax.experimental.pallas import tpu as pltpu
from jax.sharding import PartitionSpec as P

MESH = pl.DeviceIdType.MESH
F32 = jnp.float32
BF16 = jnp.bfloat16

LANES = 128
TAPS = 128
SHORT = 7
BLOCK = 128
HALO = 144
EXT = 16
WIDTH = 16
PER = LANES // WIDTH
FILT = 80
PART = 72


def ring(axis, distance):
    n = lax.axis_size(axis)
    return lax.rem(lax.axis_index(axis) + distance + n, n)


def entry_kernel(
    inputs, gates, cot, short_ref, long_ref, filt_out, in_out, gate_out, cot_out,
    mine, own_sem, send_sem, recv_sem,
):
    rows = inputs.shape[1]
    peers = lax.axis_size("fsdp")
    f = lax.axis_index("fsdp")
    after, before = ring("ctx", 1), ring("ctx", -1)
    barrier = pltpu.get_barrier_semaphore()
    for to in (after, before):
        pl.semaphore_signal(barrier, inc=1, device_id=(to, f), device_id_type=MESH)
    for d in range(1, peers):
        pl.semaphore_signal(
            barrier, inc=1, device_id=(lax.axis_index("ctx"), ring("fsdp", d)), device_id_type=MESH
        )
    mine[...] = jnp.zeros_like(mine)
    mine[0:64, :] = jnp.transpose(long_ref[...].astype(F32)).astype(BF16)
    mine[64 : 64 + SHORT, 0:64] = short_ref[...]
    pl.semaphore_wait(barrier, peers + 1)
    copies = []
    for d in range(1, peers):
        copies.append(
            pltpu.make_async_remote_copy(
                mine, filt_out.at[f], send_sem.at[d], recv_sem.at[d],
                device_id=(lax.axis_index("ctx"), ring("fsdp", d)), device_id_type=MESH,
            )
        )
    copies.append(
        pltpu.make_async_remote_copy(
            inputs.at[0, pl.ds(rows - 16, 16), :], in_out, send_sem.at[4], recv_sem.at[4],
            device_id=(after, f), device_id_type=MESH,
        )
    )
    copies.append(
        pltpu.make_async_remote_copy(
            gates.at[0, pl.ds(0, EXT), :], gate_out, send_sem.at[5], recv_sem.at[5],
            device_id=(before, f), device_id_type=MESH,
        )
    )
    copies.append(
        pltpu.make_async_remote_copy(
            cot.at[0, pl.ds(0, HALO), :], cot_out, send_sem.at[6], recv_sem.at[6],
            device_id=(before, f), device_id_type=MESH,
        )
    )
    for c in copies:
        c.start()
    own = pltpu.make_async_copy(mine, filt_out.at[f], own_sem)
    own.start()
    own.wait()
    for c in copies:
        c.wait()


def entry(inputs, gates, cot, short_filter, long_filter):
    channels = inputs.shape[2]
    peers = lax.axis_size("fsdp")
    anyspace = pl.BlockSpec(memory_space=pl.ANY)
    vmem = pl.BlockSpec(memory_space=pltpu.VMEM)
    return pl.pallas_call(
        entry_kernel,
        out_shape=(
            jax.ShapeDtypeStruct((peers, FILT, LANES), BF16),
            jax.ShapeDtypeStruct((16, channels), BF16),
            jax.ShapeDtypeStruct((EXT, channels), BF16),
            jax.ShapeDtypeStruct((HALO, channels), BF16),
        ),
        in_specs=[anyspace, anyspace, anyspace, vmem, vmem],
        out_specs=(anyspace, anyspace, anyspace, anyspace),
        scratch_shapes=[
            pltpu.VMEM((FILT, LANES), BF16),
            pltpu.SemaphoreType.DMA,
            pltpu.SemaphoreType.DMA((7,)),
            pltpu.SemaphoreType.DMA((7,)),
        ],
        compiler_params=pltpu.CompilerParams(collective_id=0, has_side_effects=True),
        name="entry",
    )(inputs, gates, cot, short_filter, long_filter)


def prepare(lengths, filt, filt32, win_mask, ext_mask, diag_mask, fwd_mask, bwd_mask, rcol, cot_s, row0):
    docs = lengths.shape[1]
    rows = fwd_mask.shape[1]
    lane_pos = row0 + lax.broadcasted_iota(jnp.int32, (8, 512), 1)
    row_pos = row0 + lax.broadcasted_iota(jnp.int32, rcol.shape, 0)

    def one_doc(d, carry):
        end, lane_start, row_start = carry
        end = end + lengths[0, d]
        return (
            end,
            jnp.where(lane_pos >= end, end, lane_start),
            jnp.where(row_pos >= end, end, row_start),
        )

    _, lane_start, row_start = lax.fori_loop(
        0, docs, one_doc,
        (jnp.int32(0), jnp.zeros((8, 512), jnp.int32), jnp.zeros(rcol.shape, jnp.int32)),
    )
    rcol[...] = (row_pos - row_start).astype(F32)
    for j in range(1, SHORT):
        fwd_mask[j - 1] = (rcol[0:rows, :] >= j).astype(F32)
        bwd_mask[j - 1] = (rcol[j : j + rows, :] >= j).astype(F32)
    s_rel = lax.broadcasted_iota(jnp.int32, (BLOCK, LANES), 0)
    lane = lax.broadcasted_iota(jnp.int32, (BLOCK, LANES), 1)
    near = lane >= s_rel
    for b in range(rows // BLOCK):
        s_abs = row0 + b * BLOCK + s_rel
        t0 = jnp.broadcast_to(lane_start[0:1, b * BLOCK : b * BLOCK + LANES], (BLOCK, LANES))
        t1 = jnp.broadcast_to(
            lane_start[0:1, (b + 1) * BLOCK : (b + 1) * BLOCK + LANES], (BLOCK, LANES)
        )
        m0 = jnp.where(near & (t0 <= s_abs), 1.0, 0.0).astype(F32)
        m1 = jnp.where(jnp.logical_not(near) & (t1 <= s_abs), 1.0, 0.0).astype(F32)
        win_mask[b, :, 0:LANES] = m0.astype(BF16)
        win_mask[b, :, LANES:] = m1.astype(BF16)
        diag_mask[b] = m0 + m1
    s_abs = row0 + rows + s_rel[0:EXT]
    t0 = jnp.broadcast_to(lane_start[0:1, rows : rows + LANES], (EXT, LANES))
    t1 = jnp.broadcast_to(lane_start[0:1, rows + LANES : rows + 2 * LANES], (EXT, LANES))
    m0 = jnp.where(near[0:EXT] & (t0 <= s_abs), 1.0, 0.0).astype(F32)
    m1 = jnp.where(jnp.logical_not(near[0:EXT]) & (t1 <= s_abs), 1.0, 0.0).astype(F32)
    ext_mask[:, 0:LANES] = m0.astype(BF16)
    ext_mask[:, LANES:] = m1.astype(BF16)
    filt32[...] = filt[...].astype(F32)
    cot_s[rows + HALO :, :] = jnp.zeros((cot_s.shape[0] - rows - HALO, LANES), BF16)


def compute_kernel(
    lengths, filt, inputs, in_before, gates, gates_after, cot, cot_after,
    gin_out, ggate_out, part_out,
    filt32, win_mask, ext_mask, diag_mask, fwd_mask, bwd_mask, rcol,
    cot_s, x_s, act_s, gate_s, ag_s, gated_m, table, ext_table, corr, back_all, back_ext,
):
    rows = inputs.shape[1]
    blocks = rows // BLOCK
    q = pl.program_id(0)
    row0 = lax.axis_index("ctx") * rows

    @pl.when(q == 0)
    def _():
        prepare(
            lengths, filt, filt32, win_mask, ext_mask, diag_mask, fwd_mask, bwd_mask, rcol, cot_s, row0
        )
        part_out[...] = jnp.zeros_like(part_out)

    per_share = 64 // PER
    share, at = q // per_share, lax.rem(q, per_share)
    lane_group = lax.broadcasted_iota(jnp.int32, (BLOCK, LANES), 1) // WIDTH
    spread = (
        lax.broadcasted_iota(jnp.int32, (LANES, LANES), 0)
        == at * PER + lax.broadcasted_iota(jnp.int32, (LANES, LANES), 1) // WIDTH
    ).astype(F32)
    taps = jnp.dot(
        filt32[share, 64:72, :].astype(BF16), spread.astype(BF16), preferred_element_type=F32
    )
    long_rows = filt32[share, pl.ds(pl.multiple_of(at * PER, PER), PER), :]

    cot_s[0:rows, :] = cot[0]
    cot_s[rows : rows + HALO, :] = cot_after[...]
    x_s[0:8, :] = in_before[...].astype(F32)[8:16]
    x_s[8:, :] = inputs[0].astype(F32)
    gate_s[0:rows, :] = gates[0].astype(F32)
    gate_s[rows:, :] = gates_after[...].astype(F32)

    act = taps[0:1, :] * x_s[8 : 8 + rows, :]
    for j in range(1, SHORT):
        act = act + fwd_mask[j - 1] * (taps[j : j + 1, :] * x_s[8 - j : 8 - j + rows, :])
    act = act.astype(BF16).astype(F32)
    act_s[...] = act
    gated = (gate_s[0:rows, :] * act).astype(BF16)

    for g in range(PER):
        circ = pltpu.roll(
            jnp.broadcast_to(long_rows[g : g + 1, :], (BLOCK, LANES)), 0, 1, stride=1, stride_axis=0
        ).astype(BF16)
        both = jnp.concatenate([circ, circ], axis=1)
        for b in range(blocks):
            table[b, g * BLOCK : (g + 1) * BLOCK, :] = both * win_mask[b]
        ext_table[g * EXT : (g + 1) * EXT, :] = both[0:EXT] * ext_mask[...]
        for b in range(blocks):
            gated_m[b, g * BLOCK : (g + 1) * BLOCK, :] = jnp.where(
                lane_group == g, gated[b * BLOCK : (b + 1) * BLOCK, :], jnp.zeros((), BF16)
            )
    for b in range(blocks):
        window = cot_s[b * BLOCK : (b + 2) * BLOCK, :]
        back_all[...] = jnp.dot(table[b], window, preferred_element_type=F32)
        back = back_all[0:BLOCK, :]
        for g in range(1, PER):
            back = jnp.where(lane_group == g, back_all[g * BLOCK : (g + 1) * BLOCK, :], back)
        own = slice(b * BLOCK, (b + 1) * BLOCK)
        ag_s[own, :] = (back * gate_s[own, :]).astype(BF16).astype(F32)
        ggate_out[0, own, :] = (back * act_s[own, :]).astype(BF16)
        corr[b] = lax.dot_general(
            gated_m[b], window, (((1,), (1,)), ((), ())), preferred_element_type=F32
        )
    back_ext[...] = jnp.dot(
        ext_table[...], cot_s[rows : rows + 2 * BLOCK, :], preferred_element_type=F32
    )
    back = back_ext[0:EXT, :]
    for g in range(1, PER):
        back = jnp.where(lane_group[0:EXT] == g, back_ext[g * EXT : (g + 1) * EXT, :], back)
    ag_s[rows:, :] = (back * gate_s[rows:, :]).astype(BF16).astype(F32)

    gin = jnp.zeros((rows, LANES), F32)
    terms = []
    for j in range(SHORT):
        moved = ag_s[j : j + rows, :]
        if j:
            moved = bwd_mask[j - 1] * moved
        gin = gin + taps[j : j + 1, :] * moved
        terms.append(jnp.sum(moved * x_s[8 : 8 + rows, :], axis=0, keepdims=True))
    gin_out[0] = gin.astype(BF16)
    terms.append(jnp.zeros((1, LANES), F32))
    gathered = (
        lax.broadcasted_iota(jnp.int32, (LANES, LANES), 1)
        == at * PER + lax.broadcasted_iota(jnp.int32, (LANES, LANES), 0) // WIDTH
    ).astype(F32)
    part_out[share, 64:72, :] += jnp.dot(
        jnp.concatenate(terms, axis=0), gathered,
        preferred_element_type=F32, precision=lax.Precision.HIGHEST,
    )

    lane8 = lax.broadcasted_iota(jnp.int32, (8, LANES), 1)
    row8 = lax.broadcasted_iota(jnp.int32, (8, LANES), 0)
    tap_rows = []
    for g in range(PER):
        total = jnp.zeros((8, LANES), F32)
        for i in range(BLOCK // 8):
            near = lane8 >= row8 + 8 * i
            at_row = g * BLOCK + 8 * i
            merged = jnp.zeros((8, LANES), F32)
            for b in range(blocks):
                merged = merged + diag_mask[b, 8 * i : 8 * i + 8, :] * jnp.where(
                    near,
                    corr[b, at_row : at_row + 8, 0:LANES],
                    corr[b, at_row : at_row + 8, LANES:],
                )
            total = total + (pltpu.roll(merged, LANES - 8 * i, 1) if i else merged)
        for bit in (1, 2, 4):
            total = jnp.where((row8 & bit) > 0, pltpu.roll(total, LANES - bit, 1), total)
        tap_rows.append(jnp.sum(total, axis=0, keepdims=True))
    part_out[share, pl.ds(pl.multiple_of(at * PER, PER), PER), :] = jnp.concatenate(
        tap_rows, axis=0
    )


def compute(lengths, filt, inputs, in_before, gates, gates_after, cot, cot_after):
    _, rows, channels = inputs.shape
    shares = filt.shape[0]
    blocks = rows // BLOCK
    whole = pl.BlockSpec((1, rows, LANES), lambda q: (0, 0, q))
    return pl.pallas_call(
        compute_kernel,
        grid=(channels // LANES,),
        out_shape=(
            jax.ShapeDtypeStruct(inputs.shape, BF16),
            jax.ShapeDtypeStruct(inputs.shape, BF16),
            jax.ShapeDtypeStruct((shares, PART, LANES), F32),
        ),
        in_specs=[
            pl.BlockSpec(memory_space=pltpu.SMEM),
            pl.BlockSpec((shares, FILT, LANES), lambda q: (0, 0, 0)),
            whole,
            pl.BlockSpec((16, LANES), lambda q: (0, q)),
            whole,
            pl.BlockSpec((EXT, LANES), lambda q: (0, q)),
            whole,
            pl.BlockSpec((HALO, LANES), lambda q: (0, q)),
        ],
        out_specs=(whole, whole, pl.BlockSpec((shares, PART, LANES), lambda q: (0, 0, 0))),
        scratch_shapes=[
            pltpu.VMEM((shares, FILT, LANES), F32),
            pltpu.VMEM((blocks, BLOCK, 2 * LANES), BF16),
            pltpu.VMEM((EXT, 2 * LANES), BF16),
            pltpu.VMEM((blocks, BLOCK, LANES), F32),
            pltpu.VMEM((SHORT - 1, rows, LANES), F32),
            pltpu.VMEM((SHORT - 1, rows, LANES), F32),
            pltpu.VMEM((rows + EXT, LANES), F32),
            pltpu.VMEM((rows + 2 * BLOCK, LANES), BF16),
            pltpu.VMEM((rows + 8, LANES), F32),
            pltpu.VMEM((rows, LANES), F32),
            pltpu.VMEM((rows + EXT, LANES), F32),
            pltpu.VMEM((rows + EXT, LANES), F32),
            pltpu.VMEM((blocks, PER * BLOCK, LANES), BF16),
            pltpu.VMEM((blocks, PER * BLOCK, 2 * LANES), BF16),
            pltpu.VMEM((PER * EXT, 2 * LANES), BF16),
            pltpu.VMEM((blocks, PER * BLOCK, 2 * LANES), F32),
            pltpu.VMEM((PER * BLOCK, LANES), F32),
            pltpu.VMEM((PER * EXT, LANES), F32),
        ],
        compiler_params=pltpu.CompilerParams(vmem_limit_bytes=40 << 20),
        name="layer_pair",
    )(lengths, filt, inputs, in_before, gates, gates_after, cot, cot_after)


def reduce_kernel(scale, part, short_out, long_out, bufs, cur, send_sem, recv_sem):
    side = 4
    f = lax.axis_index("fsdp")
    ctx = lax.axis_index("ctx")
    y, zl, x = lax.rem(ctx, side), lax.rem(ctx // side, side), ctx // (side * side)

    def peer(phase, d):
        if phase == 0:
            return (ctx, lax.rem(f + d, side))
        stride = (1, side * side, side)[phase - 1]
        at = (y, x, zl)[phase - 1]
        return (ctx + (lax.rem(at + d, side) - at) * stride, f)

    places = (f, y, x, zl)
    barrier = pltpu.get_barrier_semaphore()
    for phase in range(4):
        for d in range(1, side):
            pl.semaphore_signal(barrier, inc=1, device_id=peer(phase, d), device_id_type=MESH)
    pl.semaphore_wait(barrier, 4 * (side - 1))
    for phase in range(4):
        me = places[phase]
        copies = []
        for d in range(1, side):
            source = part.at[lax.rem(f + d, side)] if phase == 0 else cur.at[phase]
            copies.append(
                pltpu.make_async_remote_copy(
                    source, bufs.at[phase, side - d], send_sem.at[phase, d],
                    recv_sem.at[phase, side - d],
                    device_id=peer(phase, d), device_id_type=MESH,
                )
            )
        for c in copies:
            c.start()
        mine = part[f] if phase == 0 else cur[phase]
        for d in range(1, side):
            pltpu.make_async_remote_copy(
                cur.at[phase], bufs.at[phase, d], send_sem.at[phase, d], recv_sem.at[phase, d],
                device_id=peer(phase, d), device_id_type=MESH,
            ).wait_recv()
        bufs[phase, 0] = mine
        total = jnp.zeros(mine.shape, F32)
        for place in range(side):
            total = total + bufs[phase, lax.rem(place - me + side, side)]
        for c in copies:
            c.wait_send()
        if phase < 3:
            cur[phase + 1] = total
    total = total * scale
    wide = jnp.concatenate([total[0:64], jnp.zeros((64, LANES), F32)], axis=0)
    long_out[...] = jnp.transpose(wide)[:, 0:64]
    short_out[...] = total[64 : 64 + SHORT, 0:64]


def reduce(part, scale, short_shape, long_shape):
    vmem = pl.BlockSpec(memory_space=pltpu.VMEM)
    return pl.pallas_call(
        functools.partial(reduce_kernel, scale),
        out_shape=(
            jax.ShapeDtypeStruct(short_shape, F32),
            jax.ShapeDtypeStruct(long_shape, F32),
        ),
        in_specs=[vmem],
        out_specs=(vmem, vmem),
        scratch_shapes=[
            pltpu.VMEM((4, 4, PART, LANES), F32),
            pltpu.VMEM((4, PART, LANES), F32),
            pltpu.SemaphoreType.DMA((4, 4)),
            pltpu.SemaphoreType.DMA((4, 4)),
        ],
        compiler_params=pltpu.CompilerParams(collective_id=1, has_side_effects=True),
        name="sum_terms",
    )(part)


def on_device(inputs, gates, grad_out, doc_lengths, short_filter, long_filter):
    rows = inputs.shape[1]
    filt, in_before, gates_after, cot_after = entry(
        inputs, gates, grad_out, short_filter, long_filter
    )
    grad_inputs, grad_gates, part = compute(
        doc_lengths, filt, inputs, in_before, gates, gates_after, grad_out, cot_after
    )
    scale = 1.0 / math.sqrt(lax.axis_size("fsdp") * lax.axis_size("ctx") * rows)
    short_share, long_share = reduce(part, scale, short_filter.shape, long_filter.shape)
    return grad_inputs, grad_gates, short_share, long_share


def solution(mesh):
    rows = P("fsdp", "ctx", None)
    return jax.shard_map(
        on_device,
        mesh=mesh,
        in_specs=(rows, rows, rows, P("fsdp", None), P(None, "fsdp"), P(None, "fsdp")),
        out_specs=(rows, rows, P(None, "fsdp"), P(None, "fsdp")),
        check_vma=False,
    )
```

```python
import functools
import math

import jax
import jax.numpy as jnp
from jax import lax
from jax.experimental import pallas as pl
from jax.experimental.pallas import tpu as pltpu
from jax.sharding import PartitionSpec as P

MESH = pl.DeviceIdType.MESH
F32 = jnp.float32
BF16 = jnp.bfloat16

LANES = 128
TAPS = 128
SHORT = 7
BLOCK = 128
HALO = 144
EXT = 16
WIDTH = 16
PER = LANES // WIDTH
PIECES = 8
FILT = 80
PART = 80


def ring(axis, distance):
    n = lax.axis_size(axis)
    return lax.rem(lax.axis_index(axis) + distance + n, n)


def prepare(lengths, win_mask, ext_mask, diag_mask, fwd_mask, bwd_mask, rcol, row0):
    docs = lengths.shape[1]
    rows = fwd_mask.shape[1]
    lane_pos = row0 + lax.broadcasted_iota(jnp.int32, (8, 512), 1)
    row_pos = row0 + lax.broadcasted_iota(jnp.int32, rcol.shape, 0)

    def one_doc(d, carry):
        end, lane_start, row_start = carry
        end = end + lengths[0, d]
        return (
            end,
            jnp.where(lane_pos >= end, end, lane_start),
            jnp.where(row_pos >= end, end, row_start),
        )

    _, lane_start, row_start = lax.fori_loop(
        0, docs, one_doc,
        (jnp.int32(0), jnp.zeros((8, 512), jnp.int32), jnp.zeros(rcol.shape, jnp.int32)),
    )
    rcol[...] = (row_pos - row_start).astype(F32)
    for j in range(1, SHORT):
        fwd_mask[j - 1] = (rcol[0:rows, :] >= j).astype(F32)
        bwd_mask[j - 1] = (rcol[j : j + rows, :] >= j).astype(F32)
    s_rel = lax.broadcasted_iota(jnp.int32, (BLOCK, LANES), 0)
    lane = lax.broadcasted_iota(jnp.int32, (BLOCK, LANES), 1)
    near = lane >= s_rel
    for b in range(rows // BLOCK):
        s_abs = row0 + b * BLOCK + s_rel
        t0 = jnp.broadcast_to(lane_start[0:1, b * BLOCK : b * BLOCK + LANES], (BLOCK, LANES))
        t1 = jnp.broadcast_to(
            lane_start[0:1, (b + 1) * BLOCK : (b + 1) * BLOCK + LANES], (BLOCK, LANES)
        )
        m0 = jnp.where(near & (t0 <= s_abs), 1.0, 0.0).astype(F32)
        m1 = jnp.where(jnp.logical_not(near) & (t1 <= s_abs), 1.0, 0.0).astype(F32)
        win_mask[b, :, 0:LANES] = m0.astype(BF16)
        win_mask[b, :, LANES:] = m1.astype(BF16)
        diag_mask[b] = m0 + m1
    s_abs = row0 + rows + s_rel[0:EXT]
    t0 = jnp.broadcast_to(lane_start[0:1, rows : rows + LANES], (EXT, LANES))
    t1 = jnp.broadcast_to(lane_start[0:1, rows + LANES : rows + 2 * LANES], (EXT, LANES))
    m0 = jnp.where(near[0:EXT] & (t0 <= s_abs), 1.0, 0.0).astype(F32)
    m1 = jnp.where(jnp.logical_not(near[0:EXT]) & (t1 <= s_abs), 1.0, 0.0).astype(F32)
    ext_mask[:, 0:LANES] = m0.astype(BF16)
    ext_mask[:, LANES:] = m1.astype(BF16)


def chunk(q):
    return pl.ds(pl.multiple_of(q * LANES, LANES), LANES)


def lane_groups(rows):
    return lax.broadcasted_iota(jnp.int32, (rows, LANES), 1) // WIDTH


def chunk_taps(filt32, share, at):
    spread = (
        lax.broadcasted_iota(jnp.int32, (LANES, LANES), 0)
        == at * PER + lax.broadcasted_iota(jnp.int32, (LANES, LANES), 1) // WIDTH
    ).astype(F32)
    return jnp.dot(
        filt32[share, 64:72, :].astype(BF16), spread.astype(BF16), preferred_element_type=F32
    )


def pick(stacked, rows):
    group = lane_groups(rows)
    picked = stacked[0:rows, :]
    for g in range(1, PER):
        picked = jnp.where(group == g, stacked[g * rows : (g + 1) * rows, :], picked)
    return picked


def split_groups(split, gated):
    group = lane_groups(BLOCK)
    for g in range(PER):
        split[g * BLOCK : (g + 1) * BLOCK, :] = jnp.where(group == g, gated, jnp.zeros((), BF16))


def tap_sums(corr, diag):
    lane8 = lax.broadcasted_iota(jnp.int32, (8, LANES), 1)
    row8 = lax.broadcasted_iota(jnp.int32, (8, LANES), 0)
    tap_rows = []
    for g in range(PER):
        total = jnp.zeros((8, LANES), F32)
        for i in range(BLOCK // 8):
            at_row = g * BLOCK + 8 * i
            merged = diag[8 * i : 8 * i + 8, :] * jnp.where(
                lane8 >= row8 + 8 * i,
                corr[at_row : at_row + 8, 0:LANES],
                corr[at_row : at_row + 8, LANES:],
            )
            total = total + (pltpu.roll(merged, LANES - 8 * i, 1) if i else merged)
        for bit in (1, 2, 4):
            total = jnp.where((row8 & bit) > 0, pltpu.roll(total, LANES - bit, 1), total)
        tap_rows.append(jnp.sum(total, axis=0, keepdims=True))
    return jnp.concatenate(tap_rows, axis=0)


def pair_kernel(
    lengths, inputs, gates, cot, short_ref, long_ref,
    gin_out, ggate_out, part_out,
    mine, filt, filt32, x_all, before_all, g_all, cot_all, act_all, ag_all, circ_all,
    win_mask, ext_mask, diag_mask, fwd_mask, bwd_mask, rcol,
    x_s, ag_s, split, table, ext_table, corr, back_all, back_ext,
    own_sem, send_sem, recv_sem, cot_send, cot_recv,
):
    rows, channels = inputs.shape[1:]
    chunks = channels // LANES
    per_share = 64 // PER
    width = channels // PIECES
    peers = lax.axis_size("fsdp")
    f = lax.axis_index("fsdp")
    ctx = lax.axis_index("ctx")
    row0 = ctx * rows
    after, before = ring("ctx", 1), ring("ctx", -1)
    barrier = pltpu.get_barrier_semaphore()
    for to in (after, before):
        pl.semaphore_signal(barrier, inc=1, device_id=(to, f), device_id_type=MESH)
    for d in range(1, peers):
        pl.semaphore_signal(barrier, inc=1, device_id=(ctx, ring("fsdp", d)), device_id_type=MESH)
    local = [
        pltpu.make_async_copy(inputs.at[0], x_all, own_sem.at[0]),
        pltpu.make_async_copy(gates.at[0], g_all.at[pl.ds(0, rows), :], own_sem.at[1]),
        pltpu.make_async_copy(cot.at[0], cot_all.at[pl.ds(0, rows), :], own_sem.at[2]),
    ]
    for c in local:
        c.start()
    mine[...] = jnp.zeros_like(mine)
    mine[0:64, :] = long_ref[...]
    mine[64 : 64 + SHORT, 0:64] = short_ref[...]
    pl.semaphore_wait(barrier, peers + 1)
    small = []
    for d in range(1, peers):
        small.append(
            pltpu.make_async_remote_copy(
                mine, filt.at[f], send_sem.at[d], recv_sem.at[d],
                device_id=(ctx, ring("fsdp", d)), device_id_type=MESH,
            )
        )
    small.append(
        pltpu.make_async_remote_copy(
            inputs.at[0, pl.ds(rows - 16, 16), :], before_all, send_sem.at[4], recv_sem.at[4],
            device_id=(after, f), device_id_type=MESH,
        )
    )
    for c in small:
        c.start()

    def piece(p):
        lanes = pl.ds(pl.multiple_of(p * width, LANES), width)
        return pltpu.make_async_remote_copy(
            cot.at[0, pl.ds(0, HALO), lanes], cot_all.at[pl.ds(rows, HALO), lanes],
            cot_send.at[p], cot_recv.at[p],
            device_id=(before, f), device_id_type=MESH,
        )

    gate_copy = pltpu.make_async_remote_copy(
        gates.at[0, pl.ds(0, EXT), :], g_all.at[pl.ds(rows, EXT), :],
        send_sem.at[5], recv_sem.at[5],
        device_id=(before, f), device_id_type=MESH,
    )
    gate_copy.start()
    for p in range(PIECES):
        piece(p).start()

    prepare(lengths, win_mask, ext_mask, diag_mask, fwd_mask, bwd_mask, rcol, row0)
    cot_all[rows + HALO :, :] = jnp.zeros((cot_all.shape[0] - rows - HALO, channels), BF16)
    part_out[...] = jnp.zeros_like(part_out)
    filt[f] = mine[...]
    for c in small:
        c.wait_recv()
    for c in local:
        c.wait()
    filt32[...] = filt[...].astype(F32)

    def first_half(q, carry):
        lanes = chunk(q)
        share, at = q // per_share, lax.rem(q, per_share)
        taps = chunk_taps(filt32, share, at)
        own_groups = pl.ds(pl.multiple_of(at * PER, PER), PER)
        long_rows = filt32[share, own_groups, :]
        x_s[0:8, :] = before_all[:, lanes].astype(F32)[8:16]
        x_s[8:, :] = x_all[:, lanes].astype(F32)
        act = taps[0:1, :] * x_s[8 : 8 + rows, :]
        for j in range(1, SHORT):
            act = act + fwd_mask[j - 1] * (taps[j : j + 1, :] * x_s[8 - j : 8 - j + rows, :])
        act = act.astype(BF16)
        act_all[:, lanes] = act
        act = act[0:BLOCK].astype(F32)
        gate = g_all[0:BLOCK, lanes].astype(F32)
        split_groups(split, (gate * act).astype(BF16))
        for g in range(PER):
            circ = pltpu.roll(
                jnp.broadcast_to(long_rows[g : g + 1, :], (BLOCK, LANES)), 0, 1,
                stride=1, stride_axis=0,
            ).astype(BF16)
            circ_all[q, g * BLOCK : (g + 1) * BLOCK, :] = circ
            table[g * BLOCK : (g + 1) * BLOCK, 0:LANES] = circ * win_mask[0, :, 0:LANES]
            table[g * BLOCK : (g + 1) * BLOCK, LANES:] = circ * win_mask[0, :, LANES:]
        window = cot_all[0 : 2 * BLOCK, lanes]
        corr[...] = lax.dot_general(
            split[...], window, (((1,), (1,)), ((), ())), preferred_element_type=F32
        )
        back_all[...] = jnp.dot(table[...], window, preferred_element_type=F32)
        part_out[share, own_groups, :] = tap_sums(corr, diag_mask.at[0])
        back = pick(back_all, BLOCK)
        ag_all[:, lanes] = (back * gate).astype(BF16)
        ggate_out[0, 0:BLOCK, lanes] = (back * act).astype(BF16)
        return carry

    lax.fori_loop(0, chunks, first_half, 0)
    gate_copy.wait_recv()

    def second_half(q):
        lanes = chunk(q)
        share, at = q // per_share, lax.rem(q, per_share)
        taps = chunk_taps(filt32, share, at)
        own_groups = pl.ds(pl.multiple_of(at * PER, PER), PER)
        gate = g_all[BLOCK:, lanes].astype(F32)
        act = act_all[BLOCK:, lanes].astype(F32)
        split_groups(split, (gate[0:BLOCK] * act).astype(BF16))
        for g in range(PER):
            circ = circ_all[q, g * BLOCK : (g + 1) * BLOCK, :]
            table[g * BLOCK : (g + 1) * BLOCK, 0:LANES] = circ * win_mask[1, :, 0:LANES]
            table[g * BLOCK : (g + 1) * BLOCK, LANES:] = circ * win_mask[1, :, LANES:]
            ext_table[g * EXT : (g + 1) * EXT, 0:LANES] = circ[0:EXT] * ext_mask[:, 0:LANES]
            ext_table[g * EXT : (g + 1) * EXT, LANES:] = circ[0:EXT] * ext_mask[:, LANES:]
        window = cot_all[BLOCK : 3 * BLOCK, lanes]
        corr[...] = lax.dot_general(
            split[...], window, (((1,), (1,)), ((), ())), preferred_element_type=F32
        )
        back_all[...] = jnp.dot(table[...], window, preferred_element_type=F32)
        back_ext[...] = jnp.dot(
            ext_table[...], cot_all[2 * BLOCK : 4 * BLOCK, lanes], preferred_element_type=F32
        )
        part_out[share, own_groups, :] += tap_sums(corr, diag_mask.at[1])
        back = pick(back_all, BLOCK)
        ag_s[0:BLOCK, :] = ag_all[:, lanes].astype(F32)
        ag_s[BLOCK:rows, :] = (back * gate[0:BLOCK]).astype(BF16).astype(F32)
        ag_s[rows:, :] = (pick(back_ext, EXT) * gate[BLOCK:]).astype(BF16).astype(F32)
        ggate_out[0, BLOCK:, lanes] = (back * act).astype(BF16)

        x = x_all[:, lanes].astype(F32)
        gin = jnp.zeros((rows, LANES), F32)
        terms = []
        for j in range(SHORT):
            moved = ag_s[j : j + rows, :]
            if j:
                moved = bwd_mask[j - 1] * moved
            gin = gin + taps[j : j + 1, :] * moved
            terms.append(jnp.sum(moved * x, axis=0, keepdims=True))
        gin_out[0, :, lanes] = gin.astype(BF16)
        terms.append(jnp.zeros((1, LANES), F32))
        gathered = (
            lax.broadcasted_iota(jnp.int32, (LANES, LANES), 1)
            == at * PER + lax.broadcasted_iota(jnp.int32, (LANES, LANES), 0) // WIDTH
        ).astype(F32)
        part_out[share, 64:72, :] += jnp.dot(
            jnp.concatenate(terms, axis=0), gathered,
            preferred_element_type=F32, precision=lax.Precision.HIGHEST,
        )

    def one_piece(p, carry):
        piece(p).wait_recv()

        def inner(i, c):
            second_half(p * (chunks // PIECES) + i)
            return c

        return lax.fori_loop(0, chunks // PIECES, inner, carry)

    lax.fori_loop(0, PIECES, one_piece, 0)
    for c in small:
        c.wait_send()
    gate_copy.wait_send()
    for p in range(PIECES):
        piece(p).wait_send()


def layer_pair(inputs, gates, cot, lengths, short_filter, long_filter):
    _, rows, channels = inputs.shape
    assert rows == 2 * BLOCK
    shares = lax.axis_size("fsdp")
    chunks = channels // LANES
    anyspace = pl.BlockSpec(memory_space=pl.ANY)
    vmem = pl.BlockSpec(memory_space=pltpu.VMEM)
    stack = PER * BLOCK
    return pl.pallas_call(
        pair_kernel,
        out_shape=(
            jax.ShapeDtypeStruct(inputs.shape, BF16),
            jax.ShapeDtypeStruct(inputs.shape, BF16),
            jax.ShapeDtypeStruct((shares, PART, LANES), F32),
        ),
        in_specs=[pl.BlockSpec(memory_space=pltpu.SMEM), anyspace, anyspace, anyspace, vmem, vmem],
        out_specs=(vmem, vmem, vmem),
        scratch_shapes=[
            pltpu.VMEM((FILT, LANES), BF16),
            pltpu.VMEM((shares, FILT, LANES), BF16),
            pltpu.VMEM((shares, FILT, LANES), F32),
            pltpu.VMEM((rows, channels), BF16),
            pltpu.VMEM((16, channels), BF16),
            pltpu.VMEM((rows + EXT, channels), BF16),
            pltpu.VMEM((rows + 2 * BLOCK, channels), BF16),
            pltpu.VMEM((rows, channels), BF16),
            pltpu.VMEM((BLOCK, channels), BF16),
            pltpu.VMEM((chunks, stack, LANES), BF16),
            pltpu.VMEM((2, BLOCK, 2 * LANES), BF16),
            pltpu.VMEM((EXT, 2 * LANES), BF16),
            pltpu.VMEM((2, BLOCK, LANES), F32),
            pltpu.VMEM((SHORT - 1, rows, LANES), F32),
            pltpu.VMEM((SHORT - 1, rows, LANES), F32),
            pltpu.VMEM((rows + EXT, LANES), F32),
            pltpu.VMEM((rows + 8, LANES), F32),
            pltpu.VMEM((rows + EXT, LANES), F32),
            pltpu.VMEM((stack, LANES), BF16),
            pltpu.VMEM((stack, 2 * LANES), BF16),
            pltpu.VMEM((PER * EXT, 2 * LANES), BF16),
            pltpu.VMEM((stack, 2 * LANES), F32),
            pltpu.VMEM((stack, LANES), F32),
            pltpu.VMEM((PER * EXT, LANES), F32),
            pltpu.SemaphoreType.DMA((3,)),
            pltpu.SemaphoreType.DMA((6,)),
            pltpu.SemaphoreType.DMA((6,)),
            pltpu.SemaphoreType.DMA((PIECES,)),
            pltpu.SemaphoreType.DMA((PIECES,)),
        ],
        compiler_params=pltpu.CompilerParams(
            collective_id=0, has_side_effects=True, vmem_limit_bytes=56 << 20
        ),
        name="layer_pair",
    )(lengths, inputs, gates, cot, short_filter, long_filter)


def reduce_kernel(scale, part, short_out, long_out, half, landed, bufs, cur, send_sem, recv_sem):
    side = 4
    f = lax.axis_index("fsdp")
    ctx = lax.axis_index("ctx")
    core, high = lax.rem(f, 2), f // 2
    y, low, x = lax.rem(ctx, side), lax.rem(ctx // side, side), ctx // (side * side)
    core_peer = (ctx, high * 2 + 1 - core)
    high_peer = (ctx, (1 - high) * 2 + core)
    axes = ((y, 1), (x, side * side), (low, side))

    def peer(axis, d):
        at, stride = axes[axis]
        return (ctx + (lax.rem(at + d, side) - at) * stride, f)

    barrier = pltpu.get_barrier_semaphore()
    for to in [core_peer, high_peer] + [peer(a, d) for a in range(3) for d in range(1, side)]:
        pl.semaphore_signal(barrier, inc=1, device_id=to, device_id_type=MESH)
    pl.semaphore_wait(barrier, 2 + 3 * (side - 1))

    swaps = [
        pltpu.make_async_remote_copy(
            part.at[2 * h + 1 - core], half.at[h], send_sem.at[0, h], recv_sem.at[0, h],
            device_id=core_peer, device_id_type=MESH,
        )
        for h in range(2)
    ]
    for c in swaps:
        c.start()
    for c in swaps:
        c.wait_recv()
    cur[0] = (part[2 * (1 - high) + core] + half[1 - high]).astype(BF16)
    cross = pltpu.make_async_remote_copy(
        cur.at[0], landed, send_sem.at[1, 0], recv_sem.at[1, 0],
        device_id=high_peer, device_id_type=MESH,
    )
    cross.start()
    total = part[2 * high + core] + half[high]
    cross.wait_recv()
    total = total + landed[...].astype(F32)
    sent = swaps + [cross]
    for axis in range(3):
        at = axes[axis][0]
        cur[axis + 1] = total.astype(BF16)
        copies = [
            pltpu.make_async_remote_copy(
                cur.at[axis + 1], bufs.at[axis, side - d],
                send_sem.at[axis + 2, d], recv_sem.at[axis + 2, side - d],
                device_id=peer(axis, d), device_id_type=MESH,
            )
            for d in range(1, side)
        ]
        for c in copies:
            c.start()
        sent += copies
        bufs[axis, 0] = cur[axis + 1]
        for c in copies:
            c.wait_recv()
        total = jnp.zeros(total.shape, F32)
        for place in range(side):
            total = total + bufs[axis, lax.rem(place - at + side, side)].astype(F32)
    total = total * scale
    long_out[...] = total[0:64]
    short_out[...] = total[64 : 64 + SHORT, 0:64]
    for c in sent:
        c.wait_send()


def reduce(part, scale, short_shape, long_shape):
    vmem = pl.BlockSpec(memory_space=pltpu.VMEM)
    return pl.pallas_call(
        functools.partial(reduce_kernel, scale),
        out_shape=(
            jax.ShapeDtypeStruct(short_shape, F32),
            jax.ShapeDtypeStruct(long_shape, F32),
        ),
        in_specs=[vmem],
        out_specs=(vmem, vmem),
        scratch_shapes=[
            pltpu.VMEM((2, PART, LANES), F32),
            pltpu.VMEM((PART, LANES), BF16),
            pltpu.VMEM((3, 4, PART, LANES), BF16),
            pltpu.VMEM((4, PART, LANES), BF16),
            pltpu.SemaphoreType.DMA((5, 4)),
            pltpu.SemaphoreType.DMA((5, 4)),
        ],
        compiler_params=pltpu.CompilerParams(collective_id=1, has_side_effects=True),
        name="sum_terms",
    )(part)


def on_device(inputs, gates, grad_out, doc_lengths, short_filter, long_filter):
    rows = inputs.shape[1]
    grad_inputs, grad_gates, part = layer_pair(
        inputs, gates, grad_out, doc_lengths, short_filter, jnp.transpose(long_filter)
    )
    scale = 1.0 / math.sqrt(lax.axis_size("fsdp") * lax.axis_size("ctx") * rows)
    short_share, long_share = reduce(part, scale, short_filter.shape, long_filter.shape[::-1])
    return grad_inputs, grad_gates, short_share, jnp.transpose(long_share)


def solution(mesh):
    rows = P("fsdp", "ctx", None)
    return jax.shard_map(
        on_device,
        mesh=mesh,
        in_specs=(rows, rows, rows, P("fsdp", None), P(None, "fsdp"), P(None, "fsdp")),
        out_specs=(rows, rows, P(None, "fsdp"), P(None, "fsdp")),
        check_vma=False,
    )
```

```python
import functools
import math

import jax
import jax.numpy as jnp
from jax import lax
from jax.experimental import pallas as pl
from jax.experimental.pallas import tpu as pltpu
from jax.sharding import PartitionSpec as P

MESH = pl.DeviceIdType.MESH
F32 = jnp.float32
BF16 = jnp.bfloat16

LANES = 128
TAPS = 128
SHORT = 7
BLOCK = 128
SUB = 32
HALO = 144
EXT = 16
WIDTH = 16
PER = LANES // WIDTH
PARTS = 4
PIECES = 8
FILT = 80
PART = 80


def ring(axis, distance):
    n = lax.axis_size(axis)
    return lax.rem(lax.axis_index(axis) + distance + n, n)


def prepare(lengths, win_mask, ext_mask, diag_mask, fwd_mask, bwd_mask, rcol, row0):
    docs = lengths.shape[1]
    rows = fwd_mask.shape[1]
    lane_pos = row0 + lax.broadcasted_iota(jnp.int32, (8, 512), 1)

    def one_doc(d, carry):
        end, start = carry
        end = end + lengths[0, d]
        return end, jnp.where(lane_pos >= end, end, start)

    _, start = lax.fori_loop(0, docs, one_doc, (jnp.int32(0), jnp.zeros((8, 512), jnp.int32)))
    passed = (lane_pos - start).astype(F32)
    for k in range(3):
        own = slice(k * LANES, (k + 1) * LANES)
        turned = jnp.transpose(jnp.broadcast_to(passed[0:1, own], (LANES, LANES)))
        rcol[k * LANES : k * LANES + LANES, :] = turned
    for j in range(1, SHORT):
        fwd_mask[j - 1] = (rcol[0:rows, :] >= j).astype(F32)
        bwd_mask[j - 1] = (rcol[j : j + rows, :] >= j).astype(F32)
    s_rel = lax.broadcasted_iota(jnp.int32, (BLOCK, LANES), 0)
    lane = lax.broadcasted_iota(jnp.int32, (BLOCK, LANES), 1)

    def starts_at(first, count):
        return jnp.broadcast_to(start[0:1, first : first + LANES], (count, LANES))

    for b in range(rows // BLOCK):
        s_abs = row0 + b * BLOCK + s_rel
        near = lane >= s_rel
        first = b * BLOCK
        m0 = jnp.where(near & (starts_at(first, BLOCK) <= s_abs), 1.0, 0.0)
        m1 = jnp.where(near | (starts_at(first + LANES, BLOCK) > s_abs), 0.0, 1.0)
        win_mask[b, :, 0:LANES] = m0.astype(BF16)
        win_mask[b, :, LANES:] = m1.astype(BF16)
        for k in range(BLOCK // SUB):
            own = slice(k * SUB, (k + 1) * SUB)
            first = b * BLOCK + k * SUB
            near = lane[0:SUB] >= s_rel[0:SUB]
            target = jnp.where(near, starts_at(first, SUB), starts_at(first + LANES, SUB))
            diag_mask[b, own, :] = jnp.where(target <= s_abs[own], 1.0, 0.0)
    s_abs = row0 + rows + s_rel[0:EXT]
    near = (lane >= s_rel)[0:EXT]
    m0 = jnp.where(near & (starts_at(rows, EXT) <= s_abs), 1.0, 0.0)
    m1 = jnp.where(near | (starts_at(rows + LANES, EXT) > s_abs), 0.0, 1.0)
    ext_mask[:, 0:LANES] = m0.astype(BF16)
    ext_mask[:, LANES:] = m1.astype(BF16)


def chunk(q):
    return pl.ds(pl.multiple_of(q * LANES, LANES), LANES)


def lane_groups(rows):
    return lax.broadcasted_iota(jnp.int32, (rows, LANES), 1) // WIDTH


def chunk_taps(filt32, share, at):
    spread = (
        lax.broadcasted_iota(jnp.int32, (LANES, LANES), 0)
        == at * PER + lax.broadcasted_iota(jnp.int32, (LANES, LANES), 1) // WIDTH
    ).astype(F32)
    return jnp.dot(
        filt32[share, 64:72, :].astype(BF16), spread.astype(BF16), preferred_element_type=F32
    )


def pick(stacked, first, count, stride):
    group = lane_groups(count)
    picked = stacked[first : first + count, :]
    for g in range(1, PER):
        at = g * stride + first
        picked = jnp.where(group == g, stacked[at : at + count, :], picked)
    return picked


def split_groups(split, gated):
    group = lane_groups(SUB)
    for k in range(BLOCK // SUB):
        for g in range(PER):
            at = (k * PER + g) * SUB
            split[at : at + SUB, :] = jnp.where(
                group == g, gated[k * SUB : (k + 1) * SUB, :], jnp.zeros((), BF16)
            )


def correlate(corr, split, cot_all, first, lanes, k):
    own = slice(k * PER * SUB, (k + 1) * PER * SUB)
    reach = SUB + TAPS
    window = cot_all[first + k * SUB : first + k * SUB + reach, lanes]
    corr[own, 0:reach] = lax.dot_general(
        split[own, :], window, (((1,), (1,)), ((), ())), preferred_element_type=F32
    )


def merge(merged, corr, diag):
    lane8 = lax.broadcasted_iota(jnp.int32, (8, LANES), 1)
    row8 = lax.broadcasted_iota(jnp.int32, (8, LANES), 0)
    for g in range(PER):
        for i in range(SUB // 8):
            total = jnp.zeros((8, LANES), F32)
            for k in range(BLOCK // SUB):
                at_row = (k * PER + g) * SUB + 8 * i
                total = total + diag[k * SUB + 8 * i : k * SUB + 8 * i + 8, :] * jnp.where(
                    lane8 >= row8 + 8 * i,
                    corr[at_row : at_row + 8, 0:LANES],
                    corr[at_row : at_row + 8, LANES:],
                )
            merged[g * SUB + 8 * i : g * SUB + 8 * i + 8, :] = total


def line_up(merged):
    row8 = lax.broadcasted_iota(jnp.int32, (8, LANES), 0)
    tap_rows = []
    for g in range(PER):
        total = merged[g * SUB : g * SUB + 8, :]
        for i in range(1, SUB // 8):
            at = g * SUB + 8 * i
            total = total + pltpu.roll(merged[at : at + 8, :], LANES - 8 * i, 1)
        for bit in (1, 2, 4):
            total = jnp.where((row8 & bit) > 0, pltpu.roll(total, LANES - bit, 1), total)
        tap_rows.append(jnp.sum(total, axis=0, keepdims=True))
    return jnp.concatenate(tap_rows, axis=0)


def pair_kernel(
    lengths, inputs, gates, cot, short_ref, long_ref,
    gin_out, ggate_out, part_out,
    mine, filt, filt32, x_all, before_all, g_all, cot_all, act_all, ag_all, circ_all,
    win_mask, ext_mask, diag_mask, fwd_mask, bwd_mask, rcol,
    x_s, act_next, act_s, terms, merged, ag_s, split, table, ext_table, corr, back_all, back_ext,
    own_sem, send_sem, recv_sem, cot_send, cot_recv,
):
    rows, channels = inputs.shape[1:]
    chunks = channels // LANES
    per_share = 64 // PER
    width = channels // PIECES
    peers = lax.axis_size("fsdp")
    f = lax.axis_index("fsdp")
    ctx = lax.axis_index("ctx")
    row0 = ctx * rows
    after, before = ring("ctx", 1), ring("ctx", -1)
    barrier = pltpu.get_barrier_semaphore()
    for to in (after, before):
        pl.semaphore_signal(barrier, inc=1, device_id=(to, f), device_id_type=MESH)
    for d in range(1, peers):
        pl.semaphore_signal(barrier, inc=1, device_id=(ctx, ring("fsdp", d)), device_id_type=MESH)
    local = [
        pltpu.make_async_copy(inputs.at[0], x_all, own_sem.at[0]),
        pltpu.make_async_copy(gates.at[0], g_all.at[pl.ds(0, rows), :], own_sem.at[1]),
        pltpu.make_async_copy(cot.at[0], cot_all.at[pl.ds(0, rows), :], own_sem.at[2]),
    ]
    for c in local:
        c.start()
    mine[...] = jnp.zeros_like(mine)
    mine[0:64, :] = long_ref[...]
    mine[64 : 64 + SHORT, 0:64] = short_ref[...]
    pl.semaphore_wait(barrier, peers + 1)
    small = []
    for d in range(1, peers):
        small.append(
            pltpu.make_async_remote_copy(
                mine, filt.at[f], send_sem.at[d], recv_sem.at[d],
                device_id=(ctx, ring("fsdp", d)), device_id_type=MESH,
            )
        )
    small.append(
        pltpu.make_async_remote_copy(
            inputs.at[0, pl.ds(rows - 16, 16), :], before_all, send_sem.at[4], recv_sem.at[4],
            device_id=(after, f), device_id_type=MESH,
        )
    )
    for c in small:
        c.start()

    def piece(p):
        lanes = pl.ds(pl.multiple_of(p * width, LANES), width)
        return pltpu.make_async_remote_copy(
            cot.at[0, pl.ds(0, HALO), lanes], cot_all.at[pl.ds(rows, HALO), lanes],
            cot_send.at[p], cot_recv.at[p],
            device_id=(before, f), device_id_type=MESH,
        )

    gate_copy = pltpu.make_async_remote_copy(
        gates.at[0, pl.ds(0, EXT), :], g_all.at[pl.ds(rows, EXT), :],
        send_sem.at[5], recv_sem.at[5],
        device_id=(before, f), device_id_type=MESH,
    )
    gate_copy.start()
    for p in range(PIECES):
        piece(p).start()

    prepare(lengths, win_mask, ext_mask, diag_mask, fwd_mask, bwd_mask, rcol, row0)
    cot_all[rows + HALO :, :] = jnp.zeros((cot_all.shape[0] - rows - HALO, channels), BF16)
    part_out[...] = jnp.zeros_like(part_out)
    filt[f] = mine[...]
    for c in small:
        c.wait_recv()
    for c in local:
        c.wait()
    filt32[...] = filt[...].astype(F32)

    def place(q):
        share, at = q // per_share, lax.rem(q, per_share)
        return share, at, pl.ds(pl.multiple_of(at * PER, PER), PER)

    def load_next(q):
        lanes = chunk(q)
        x_s[0:8, :] = before_all[:, lanes].astype(F32)[8:16]
        x_s[8:, :] = x_all[:, lanes].astype(F32)

    def forward(q, taps, part):
        lanes = chunk(q)
        size = rows // PARTS
        own = slice(part * size, (part + 1) * size)
        act = taps[0:1, :] * x_s[8 + part * size : 8 + (part + 1) * size, :]
        for j in range(1, SHORT):
            at = 8 - j + part * size
            act = act + fwd_mask[j - 1, own, :] * (taps[j : j + 1, :] * x_s[at : at + size, :])
        act = act.astype(BF16)
        act_all[own, lanes] = act
        if (part + 1) * size <= BLOCK:
            act_next[own, :] = act.astype(F32)

    def taps_of(q):
        share, at, _ = place(q)
        return chunk_taps(filt32, share, at)

    def add_taps(q):
        share, _, own_groups = place(q)
        part_out[share, own_groups, :] += line_up(merged)

    merged[...] = jnp.zeros_like(merged)
    load_next(0)
    for part in range(PARTS):
        forward(0, taps_of(0), part)

    def first_half(q, carry):
        lanes = chunk(q)
        share, at, own_groups = place(q)
        long_rows = filt32[share, own_groups, :]
        add_taps(lax.rem(q + chunks - 1, chunks))
        gate = g_all[0:BLOCK, lanes].astype(F32)
        act = act_next[...]
        act_s[...] = act
        split_groups(split, (gate * act).astype(BF16))
        later = jnp.minimum(q + 1, chunks - 1)
        taps = taps_of(later)
        load_next(later)
        window = cot_all[0 : 2 * BLOCK, lanes]
        for part in range(PARTS):
            for g in range(part * PER // PARTS, (part + 1) * PER // PARTS):
                own = slice(g * BLOCK, (g + 1) * BLOCK)
                circ = pltpu.roll(
                    jnp.broadcast_to(long_rows[g : g + 1, :], (BLOCK, LANES)), 0, 1,
                    stride=1, stride_axis=0,
                ).astype(BF16)
                circ_all[q, own, :] = circ
                table[own, 0:LANES] = circ * win_mask[0, :, 0:LANES]
                table[own, LANES:] = circ * win_mask[0, :, LANES:]
            correlate(corr, split, cot_all, 0, lanes, part)
            own = slice(part * PER // PARTS * BLOCK, (part + 1) * PER // PARTS * BLOCK)
            back_all[own, :] = jnp.dot(table[own, :], window, preferred_element_type=F32)
            forward(later, taps, part)
        merge(merged, corr, diag_mask.at[0])
        for part in range(PARTS):
            own = slice(part * SUB, (part + 1) * SUB)
            back = pick(back_all, part * SUB, SUB, BLOCK)
            ag_all[own, lanes] = (back * g_all[own, lanes].astype(F32)).astype(BF16)
            ggate_out[0, own, lanes] = (back * act_s[own, :]).astype(BF16)
        return carry

    lax.fori_loop(0, chunks, first_half, 0)
    gate_copy.wait_recv()

    ag_s[...] = jnp.zeros_like(ag_s)

    def short_back(q, taps, part):
        lanes = chunk(q)
        size = rows // PARTS
        first = part * size
        own = slice(first, first + size)
        x = x_all[own, lanes].astype(F32)
        gin = jnp.zeros((size, LANES), F32)
        for j in range(SHORT):
            moved = ag_s[first + j : first + j + size, :]
            if j:
                moved = bwd_mask[j - 1, own, :] * moved
            gin = gin + taps[j : j + 1, :] * moved
            product = jnp.sum((moved * x).reshape(size // 8, 8, LANES), axis=0)
            if part:
                product = product + terms[8 * j : 8 * j + 8, :]
            terms[8 * j : 8 * j + 8, :] = product
        gin_out[0, own, lanes] = gin.astype(BF16)

    def short_terms(q):
        share, at, _ = place(q)
        sums = [
            jnp.sum(terms[8 * j : 8 * j + 8, :], axis=0, keepdims=True) for j in range(SHORT)
        ] + [jnp.zeros((1, LANES), F32)]
        gathered = (
            lax.broadcasted_iota(jnp.int32, (LANES, LANES), 1)
            == at * PER + lax.broadcasted_iota(jnp.int32, (LANES, LANES), 0) // WIDTH
        ).astype(F32)
        part_out[share, 64:72, :] += jnp.dot(
            jnp.concatenate(sums, axis=0), gathered,
            preferred_element_type=F32, precision=lax.Precision.HIGHEST,
        )

    def second_half(q):
        add_taps(lax.rem(q + chunks - 1, chunks))
        earlier = jnp.maximum(q - 1, 0)
        taps = taps_of(earlier)
        lanes = chunk(q)
        share, at, own_groups = place(q)
        split_groups(
            split,
            (g_all[BLOCK:rows, lanes].astype(F32) * act_all[BLOCK:, lanes].astype(F32)).astype(BF16),
        )
        window = cot_all[BLOCK : 3 * BLOCK, lanes]
        for part in range(PARTS):
            for g in range(part * PER // PARTS, (part + 1) * PER // PARTS):
                own = slice(g * BLOCK, (g + 1) * BLOCK)
                ext = slice(g * EXT, (g + 1) * EXT)
                circ = circ_all[q, own, :]
                table[own, 0:LANES] = circ * win_mask[1, :, 0:LANES]
                table[own, LANES:] = circ * win_mask[1, :, LANES:]
                ext_table[ext, 0:LANES] = circ[0:EXT] * ext_mask[:, 0:LANES]
                ext_table[ext, LANES:] = circ[0:EXT] * ext_mask[:, LANES:]
            correlate(corr, split, cot_all, BLOCK, lanes, part)
            own = slice(part * PER // PARTS * BLOCK, (part + 1) * PER // PARTS * BLOCK)
            back_all[own, :] = jnp.dot(table[own, :], window, preferred_element_type=F32)
            short_back(earlier, taps, part)
        back_ext[...] = jnp.dot(
            ext_table[...], cot_all[2 * BLOCK : 4 * BLOCK, lanes], preferred_element_type=F32
        )
        short_terms(earlier)
        merge(merged, corr, diag_mask.at[1])
        ag_s[0:BLOCK, :] = ag_all[:, lanes].astype(F32)
        for part in range(PARTS):
            own = slice(BLOCK + part * SUB, BLOCK + (part + 1) * SUB)
            back = pick(back_all, part * SUB, SUB, BLOCK)
            ag_s[own, :] = (back * g_all[own, lanes].astype(F32)).astype(BF16).astype(F32)
            ggate_out[0, own, lanes] = (back * act_all[own, lanes].astype(F32)).astype(BF16)
        back = pick(back_ext, 0, EXT, EXT)
        ag_s[rows:, :] = (back * g_all[rows:, lanes].astype(F32)).astype(BF16).astype(F32)

    def one_piece(p, carry):
        piece(p).wait_recv()

        def inner(i, c):
            second_half(p * (chunks // PIECES) + i)
            return c

        return lax.fori_loop(0, chunks // PIECES, inner, carry)

    lax.fori_loop(0, PIECES, one_piece, 0)
    taps = taps_of(chunks - 1)
    for part in range(PARTS):
        short_back(chunks - 1, taps, part)
    short_terms(chunks - 1)
    add_taps(chunks - 1)
    for c in small:
        c.wait_send()
    gate_copy.wait_send()
    for p in range(PIECES):
        piece(p).wait_send()


def layer_pair(inputs, gates, cot, lengths, short_filter, long_filter):
    _, rows, channels = inputs.shape
    assert rows == 2 * BLOCK
    shares = lax.axis_size("fsdp")
    chunks = channels // LANES
    anyspace = pl.BlockSpec(memory_space=pl.ANY)
    vmem = pl.BlockSpec(memory_space=pltpu.VMEM)
    stack = PER * BLOCK
    return pl.pallas_call(
        pair_kernel,
        out_shape=(
            jax.ShapeDtypeStruct(inputs.shape, BF16),
            jax.ShapeDtypeStruct(inputs.shape, BF16),
            jax.ShapeDtypeStruct((shares, PART, LANES), F32),
        ),
        in_specs=[pl.BlockSpec(memory_space=pltpu.SMEM), anyspace, anyspace, anyspace, vmem, vmem],
        out_specs=(vmem, vmem, vmem),
        scratch_shapes=[
            pltpu.VMEM((FILT, LANES), BF16),
            pltpu.VMEM((shares, FILT, LANES), BF16),
            pltpu.VMEM((shares, FILT, LANES), F32),
            pltpu.VMEM((rows, channels), BF16),
            pltpu.VMEM((16, channels), BF16),
            pltpu.VMEM((rows + EXT, channels), BF16),
            pltpu.VMEM((rows + 2 * BLOCK, channels), BF16),
            pltpu.VMEM((rows, channels), BF16),
            pltpu.VMEM((BLOCK, channels), BF16),
            pltpu.VMEM((chunks, stack, LANES), BF16),
            pltpu.VMEM((2, BLOCK, 2 * LANES), BF16),
            pltpu.VMEM((EXT, 2 * LANES), BF16),
            pltpu.VMEM((2, BLOCK, LANES), F32),
            pltpu.VMEM((SHORT - 1, rows, LANES), F32),
            pltpu.VMEM((SHORT - 1, rows, LANES), F32),
            pltpu.VMEM((rows + LANES, LANES), F32),
            pltpu.VMEM((rows + 8, LANES), F32),
            pltpu.VMEM((BLOCK, LANES), F32),
            pltpu.VMEM((BLOCK, LANES), F32),
            pltpu.VMEM((8 * SHORT, LANES), F32),
            pltpu.VMEM((PER * SUB, LANES), F32),
            pltpu.VMEM((rows + EXT, LANES), F32),
            pltpu.VMEM((stack, LANES), BF16),
            pltpu.VMEM((stack, 2 * LANES), BF16),
            pltpu.VMEM((PER * EXT, 2 * LANES), BF16),
            pltpu.VMEM((stack, 2 * LANES), F32),
            pltpu.VMEM((stack, LANES), F32),
            pltpu.VMEM((PER * EXT, LANES), F32),
            pltpu.SemaphoreType.DMA((3,)),
            pltpu.SemaphoreType.DMA((6,)),
            pltpu.SemaphoreType.DMA((6,)),
            pltpu.SemaphoreType.DMA((PIECES,)),
            pltpu.SemaphoreType.DMA((PIECES,)),
        ],
        compiler_params=pltpu.CompilerParams(
            collective_id=0, has_side_effects=True, vmem_limit_bytes=56 << 20
        ),
        name="layer_pair",
    )(lengths, inputs, gates, cot, short_filter, long_filter)


def reduce_kernel(scale, part, short_out, long_out, half, landed, bufs, cur, send_sem, recv_sem):
    side = 4
    f = lax.axis_index("fsdp")
    ctx = lax.axis_index("ctx")
    core, high = lax.rem(f, 2), f // 2
    y, low, x = lax.rem(ctx, side), lax.rem(ctx // side, side), ctx // (side * side)
    core_peer = (ctx, high * 2 + 1 - core)
    high_peer = (ctx, (1 - high) * 2 + core)
    axes = ((y, 1), (x, side * side), (low, side))

    def peer(axis, d):
        at, stride = axes[axis]
        return (ctx + (lax.rem(at + d, side) - at) * stride, f)

    barrier = pltpu.get_barrier_semaphore()
    for to in [core_peer, high_peer] + [peer(a, d) for a in range(3) for d in range(1, side)]:
        pl.semaphore_signal(barrier, inc=1, device_id=to, device_id_type=MESH)
    pl.semaphore_wait(barrier, 2 + 3 * (side - 1))

    swaps = [
        pltpu.make_async_remote_copy(
            part.at[2 * h + 1 - core], half.at[h], send_sem.at[0, h], recv_sem.at[0, h],
            device_id=core_peer, device_id_type=MESH,
        )
        for h in range(2)
    ]
    for c in swaps:
        c.start()
    for c in swaps:
        c.wait_recv()
    cur[0] = (part[2 * (1 - high) + core] + half[1 - high]).astype(BF16)
    cross = pltpu.make_async_remote_copy(
        cur.at[0], landed, send_sem.at[1, 0], recv_sem.at[1, 0],
        device_id=high_peer, device_id_type=MESH,
    )
    cross.start()
    total = part[2 * high + core] + half[high]
    cross.wait_recv()
    total = total + landed[...].astype(F32)
    sent = swaps + [cross]
    for axis in range(3):
        at = axes[axis][0]
        cur[axis + 1] = total.astype(BF16)
        copies = [
            pltpu.make_async_remote_copy(
                cur.at[axis + 1], bufs.at[axis, side - d],
                send_sem.at[axis + 2, d], recv_sem.at[axis + 2, side - d],
                device_id=peer(axis, d), device_id_type=MESH,
            )
            for d in range(1, side)
        ]
        for c in copies:
            c.start()
        sent += copies
        bufs[axis, 0] = cur[axis + 1]
        for c in copies:
            c.wait_recv()
        total = jnp.zeros(total.shape, F32)
        for place in range(side):
            total = total + bufs[axis, lax.rem(place - at + side, side)].astype(F32)
    total = total * scale
    long_out[...] = total[0:64]
    short_out[...] = total[64 : 64 + SHORT, 0:64]
    for c in sent:
        c.wait_send()


def reduce(part, scale, short_shape, long_shape):
    vmem = pl.BlockSpec(memory_space=pltpu.VMEM)
    return pl.pallas_call(
        functools.partial(reduce_kernel, scale),
        out_shape=(
            jax.ShapeDtypeStruct(short_shape, F32),
            jax.ShapeDtypeStruct(long_shape, F32),
        ),
        in_specs=[vmem],
        out_specs=(vmem, vmem),
        scratch_shapes=[
            pltpu.VMEM((2, PART, LANES), F32),
            pltpu.VMEM((PART, LANES), BF16),
            pltpu.VMEM((3, 4, PART, LANES), BF16),
            pltpu.VMEM((4, PART, LANES), BF16),
            pltpu.SemaphoreType.DMA((5, 4)),
            pltpu.SemaphoreType.DMA((5, 4)),
        ],
        compiler_params=pltpu.CompilerParams(collective_id=1, has_side_effects=True),
        name="sum_terms",
    )(part)


def on_device(inputs, gates, grad_out, doc_lengths, short_filter, long_filter):
    rows = inputs.shape[1]
    grad_inputs, grad_gates, part = layer_pair(
        inputs, gates, grad_out, doc_lengths, short_filter, jnp.transpose(long_filter)
    )
    scale = 1.0 / math.sqrt(lax.axis_size("fsdp") * lax.axis_size("ctx") * rows)
    short_share, long_share = reduce(part, scale, short_filter.shape, long_filter.shape[::-1])
    return grad_inputs, grad_gates, short_share, jnp.transpose(long_share)


def solution(mesh):
    rows = P("fsdp", "ctx", None)
    return jax.shard_map(
        on_device,
        mesh=mesh,
        in_specs=(rows, rows, rows, P("fsdp", None), P(None, "fsdp"), P(None, "fsdp")),
        out_specs=(rows, rows, P(None, "fsdp"), P(None, "fsdp")),
        check_vma=False,
    )
```

```python
import functools
import math

import jax
import jax.numpy as jnp
from jax import lax
from jax.experimental import pallas as pl
from jax.experimental.pallas import tpu as pltpu
from jax.sharding import PartitionSpec as P

MESH = pl.DeviceIdType.MESH
F32 = jnp.float32
BF16 = jnp.bfloat16

LANES = 128
TAPS = 128
SHORT = 7
BLOCK = 128
SUB = 32
HALO = 144
EXT = 16
WIDTH = 16
PER = LANES // WIDTH
PARTS = 4
PIECES = 8
FILT = 80
PART = 80


def ring(axis, distance):
    n = lax.axis_size(axis)
    return lax.rem(lax.axis_index(axis) + distance + n, n)


def prepare(lengths, win_mask, ext_mask, diag_mask, fwd_mask, bwd_mask, rcol, row0):
    docs = lengths.shape[1]
    rows = fwd_mask.shape[1]
    lane_pos = row0 + lax.broadcasted_iota(jnp.int32, (8, 512), 1)

    def one_doc(d, carry):
        end, start = carry
        end = end + lengths[0, d]
        return end, jnp.where(lane_pos >= end, end, start)

    _, start = lax.fori_loop(0, docs, one_doc, (jnp.int32(0), jnp.zeros((8, 512), jnp.int32)))
    passed = (lane_pos - start).astype(F32)
    for k in range(3):
        own = slice(k * LANES, (k + 1) * LANES)
        turned = jnp.transpose(jnp.broadcast_to(passed[0:1, own], (LANES, LANES)))
        rcol[k * LANES : k * LANES + LANES, :] = turned
    for j in range(1, SHORT):
        fwd_mask[j - 1] = (rcol[0:rows, :] >= j).astype(F32)
        bwd_mask[j - 1] = (rcol[j : j + rows, :] >= j).astype(F32)
    s_rel = lax.broadcasted_iota(jnp.int32, (BLOCK, LANES), 0)
    lane = lax.broadcasted_iota(jnp.int32, (BLOCK, LANES), 1)

    def starts_at(first, count):
        return jnp.broadcast_to(start[0:1, first : first + LANES], (count, LANES))

    for b in range(rows // BLOCK):
        s_abs = row0 + b * BLOCK + s_rel
        near = lane >= s_rel
        first = b * BLOCK
        m0 = jnp.where(near & (starts_at(first, BLOCK) <= s_abs), 1.0, 0.0)
        m1 = jnp.where(near | (starts_at(first + LANES, BLOCK) > s_abs), 0.0, 1.0)
        win_mask[b, :, 0:LANES] = m0.astype(BF16)
        win_mask[b, :, LANES:] = m1.astype(BF16)
        for k in range(BLOCK // SUB):
            own = slice(k * SUB, (k + 1) * SUB)
            first = b * BLOCK + k * SUB
            near = lane[0:SUB] >= s_rel[0:SUB]
            target = jnp.where(near, starts_at(first, SUB), starts_at(first + LANES, SUB))
            diag_mask[b, own, :] = jnp.where(target <= s_abs[own], 1.0, 0.0)
    s_abs = row0 + rows + s_rel[0:EXT]
    near = (lane >= s_rel)[0:EXT]
    m0 = jnp.where(near & (starts_at(rows, EXT) <= s_abs), 1.0, 0.0)
    m1 = jnp.where(near | (starts_at(rows + LANES, EXT) > s_abs), 0.0, 1.0)
    ext_mask[:, 0:LANES] = m0.astype(BF16)
    ext_mask[:, LANES:] = m1.astype(BF16)


def chunk(q):
    return pl.ds(pl.multiple_of(q * LANES, LANES), LANES)


def lane_groups(rows):
    return lax.broadcasted_iota(jnp.int32, (rows, LANES), 1) // WIDTH


def chunk_taps(filt32, share, at):
    spread = (
        lax.broadcasted_iota(jnp.int32, (LANES, LANES), 0)
        == at * PER + lax.broadcasted_iota(jnp.int32, (LANES, LANES), 1) // WIDTH
    ).astype(F32)
    return jnp.dot(
        filt32[share, 64:72, :].astype(BF16), spread.astype(BF16), preferred_element_type=F32
    )


def pick(stacked, first, count, stride):
    group = lane_groups(count)
    picked = stacked[first : first + count, :]
    for g in range(1, PER):
        at = g * stride + first
        picked = jnp.where(group == g, stacked[at : at + count, :], picked)
    return picked


def split_groups(split, gated):
    group = lane_groups(SUB)
    for k in range(BLOCK // SUB):
        for g in range(PER):
            at = (k * PER + g) * SUB
            split[at : at + SUB, :] = jnp.where(
                group == g, gated[k * SUB : (k + 1) * SUB, :], jnp.zeros((), BF16)
            )


def correlate(corr, split, cot_all, first, lanes, k):
    own = slice(k * PER * SUB, (k + 1) * PER * SUB)
    reach = SUB + TAPS
    window = cot_all[first + k * SUB : first + k * SUB + reach, lanes]
    corr[own, 0:reach] = lax.dot_general(
        split[own, :], window, (((1,), (1,)), ((), ())), preferred_element_type=F32
    )


def merge(merged, corr, diag):
    lane8 = lax.broadcasted_iota(jnp.int32, (8, LANES), 1)
    row8 = lax.broadcasted_iota(jnp.int32, (8, LANES), 0)
    for g in range(PER):
        for i in range(SUB // 8):
            total = jnp.zeros((8, LANES), F32)
            for k in range(BLOCK // SUB):
                at_row = (k * PER + g) * SUB + 8 * i
                total = total + diag[k * SUB + 8 * i : k * SUB + 8 * i + 8, :] * jnp.where(
                    lane8 >= row8 + 8 * i,
                    corr[at_row : at_row + 8, 0:LANES],
                    corr[at_row : at_row + 8, LANES:],
                )
            merged[g * SUB + 8 * i : g * SUB + 8 * i + 8, :] = total


def line_up(merged):
    row8 = lax.broadcasted_iota(jnp.int32, (8, LANES), 0)
    tap_rows = []
    for g in range(PER):
        total = merged[g * SUB : g * SUB + 8, :]
        for i in range(1, SUB // 8):
            at = g * SUB + 8 * i
            total = total + pltpu.roll(merged[at : at + 8, :], LANES - 8 * i, 1)
        for bit in (1, 2, 4):
            total = jnp.where((row8 & bit) > 0, pltpu.roll(total, LANES - bit, 1), total)
        tap_rows.append(jnp.sum(total, axis=0, keepdims=True))
    return jnp.concatenate(tap_rows, axis=0)


def pair_kernel(
    lengths, inputs, gates, cot, short_ref, long_ref,
    gin_out, ggate_out, part_out,
    mine, filt, filt32, x_all, before_all, g_all, cot_all, act_all, ag_all, circ_all,
    win_mask, ext_mask, diag_mask, fwd_mask, bwd_mask, rcol,
    x_s, act_next, act_s, terms, merged, ag_s, split, table, ext_table, corr, back_all, back_ext,
    own_sem, send_sem, recv_sem, cot_send, cot_recv,
):
    rows, channels = inputs.shape[1:]
    chunks = channels // LANES
    per_share = 64 // PER
    width = channels // PIECES
    peers = lax.axis_size("fsdp")
    f = lax.axis_index("fsdp")
    ctx = lax.axis_index("ctx")
    row0 = ctx * rows
    after, before = ring("ctx", 1), ring("ctx", -1)
    barrier = pltpu.get_barrier_semaphore()
    for to in (after, before):
        pl.semaphore_signal(barrier, inc=1, device_id=(to, f), device_id_type=MESH)
    for d in range(1, peers):
        pl.semaphore_signal(barrier, inc=1, device_id=(ctx, ring("fsdp", d)), device_id_type=MESH)
    local = [
        pltpu.make_async_copy(inputs.at[0], x_all, own_sem.at[0]),
        pltpu.make_async_copy(gates.at[0], g_all.at[pl.ds(0, rows), :], own_sem.at[1]),
        pltpu.make_async_copy(cot.at[0], cot_all.at[pl.ds(0, rows), :], own_sem.at[2]),
    ]
    for c in local:
        c.start()
    mine[...] = jnp.zeros_like(mine)
    mine[0:64, :] = long_ref[...]
    mine[64 : 64 + SHORT, 0:64] = short_ref[...]
    pl.semaphore_wait(barrier, peers + 1)
    small = []
    for d in range(1, peers):
        small.append(
            pltpu.make_async_remote_copy(
                mine, filt.at[f], send_sem.at[d], recv_sem.at[d],
                device_id=(ctx, ring("fsdp", d)), device_id_type=MESH,
            )
        )
    small.append(
        pltpu.make_async_remote_copy(
            inputs.at[0, pl.ds(rows - 16, 16), :], before_all, send_sem.at[4], recv_sem.at[4],
            device_id=(after, f), device_id_type=MESH,
        )
    )
    for c in small:
        c.start()

    def piece(p):
        lanes = pl.ds(pl.multiple_of(p * width, LANES), width)
        return pltpu.make_async_remote_copy(
            cot.at[0, pl.ds(0, HALO), lanes], cot_all.at[pl.ds(rows, HALO), lanes],
            cot_send.at[p], cot_recv.at[p],
            device_id=(before, f), device_id_type=MESH,
        )

    gate_copy = pltpu.make_async_remote_copy(
        gates.at[0, pl.ds(0, EXT), :], g_all.at[pl.ds(rows, EXT), :],
        send_sem.at[5], recv_sem.at[5],
        device_id=(before, f), device_id_type=MESH,
    )
    gate_copy.start()
    for p in range(PIECES):
        piece(p).start()

    prepare(lengths, win_mask, ext_mask, diag_mask, fwd_mask, bwd_mask, rcol, row0)
    cot_all[rows + HALO :, :] = jnp.zeros((cot_all.shape[0] - rows - HALO, channels), BF16)
    part_out[...] = jnp.zeros_like(part_out)
    filt[f] = mine[...]
    for c in small:
        c.wait_recv()
    for c in local:
        c.wait()
    filt32[...] = filt[...].astype(F32)

    def place(q):
        share, at = q // per_share, lax.rem(q, per_share)
        return share, at, pl.ds(pl.multiple_of(at * PER, PER), PER)

    def load_next(q):
        lanes = chunk(q)
        x_s[0:8, :] = before_all[:, lanes].astype(F32)[8:16]
        x_s[8:, :] = x_all[:, lanes].astype(F32)

    def forward(q, taps, part):
        lanes = chunk(q)
        size = rows // PARTS
        own = slice(part * size, (part + 1) * size)
        act = taps[0:1, :] * x_s[8 + part * size : 8 + (part + 1) * size, :]
        for j in range(1, SHORT):
            at = 8 - j + part * size
            act = act + fwd_mask[j - 1, own, :] * (taps[j : j + 1, :] * x_s[at : at + size, :])
        act = act.astype(BF16)
        act_all[own, lanes] = act
        if (part + 1) * size <= BLOCK:
            act_next[own, :] = act.astype(F32)

    def taps_of(q):
        share, at, _ = place(q)
        return chunk_taps(filt32, share, at)

    def add_taps(q):
        share, _, own_groups = place(q)
        part_out[share, own_groups, :] += line_up(merged)

    merged[...] = jnp.zeros_like(merged)
    load_next(0)
    for part in range(PARTS):
        forward(0, taps_of(0), part)

    def first_half(q, carry):
        lanes = chunk(q)
        share, at, own_groups = place(q)
        long_rows = filt32[share, own_groups, :]
        add_taps(lax.rem(q + chunks - 1, chunks))
        gate = g_all[0:BLOCK, lanes].astype(F32)
        act = act_next[...]
        act_s[...] = act
        split_groups(split, (gate * act).astype(BF16))
        later = jnp.minimum(q + 1, chunks - 1)
        taps = taps_of(later)
        load_next(later)
        window = cot_all[0 : 2 * BLOCK, lanes]
        for part in range(PARTS):
            for g in range(part * PER // PARTS, (part + 1) * PER // PARTS):
                own = slice(g * BLOCK, (g + 1) * BLOCK)
                circ = pltpu.roll(
                    jnp.broadcast_to(long_rows[g : g + 1, :], (BLOCK, LANES)), 0, 1,
                    stride=1, stride_axis=0,
                ).astype(BF16)
                circ_all[q, own, :] = circ
                table[own, 0:LANES] = circ * win_mask[0, :, 0:LANES]
                table[own, LANES:] = circ * win_mask[0, :, LANES:]
            correlate(corr, split, cot_all, 0, lanes, part)
            own = slice(part * PER // PARTS * BLOCK, (part + 1) * PER // PARTS * BLOCK)
            back_all[own, :] = jnp.dot(table[own, :], window, preferred_element_type=F32)
            forward(later, taps, part)
        merge(merged, corr, diag_mask.at[0])
        for part in range(PARTS):
            own = slice(part * SUB, (part + 1) * SUB)
            back = pick(back_all, part * SUB, SUB, BLOCK)
            ag_all[own, lanes] = (back * g_all[own, lanes].astype(F32)).astype(BF16)
            ggate_out[0, own, lanes] = (back * act_s[own, :]).astype(BF16)
        return carry

    lax.fori_loop(0, chunks, first_half, 0)
    gate_copy.wait_recv()

    ag_s[...] = jnp.zeros_like(ag_s)

    def short_back(q, taps, part):
        lanes = chunk(q)
        size = rows // PARTS
        first = part * size
        own = slice(first, first + size)
        x = x_all[own, lanes].astype(F32)
        gin = jnp.zeros((size, LANES), F32)
        for j in range(SHORT):
            moved = ag_s[first + j : first + j + size, :]
            if j:
                moved = bwd_mask[j - 1, own, :] * moved
            gin = gin + taps[j : j + 1, :] * moved
            product = jnp.sum((moved * x).reshape(size // 8, 8, LANES), axis=0)
            if part:
                product = product + terms[8 * j : 8 * j + 8, :]
            terms[8 * j : 8 * j + 8, :] = product
        gin_out[0, own, lanes] = gin.astype(BF16)

    def short_terms(q):
        share, at, _ = place(q)
        sums = [
            jnp.sum(terms[8 * j : 8 * j + 8, :], axis=0, keepdims=True) for j in range(SHORT)
        ] + [jnp.zeros((1, LANES), F32)]
        gathered = (
            lax.broadcasted_iota(jnp.int32, (LANES, LANES), 1)
            == at * PER + lax.broadcasted_iota(jnp.int32, (LANES, LANES), 0) // WIDTH
        ).astype(F32)
        part_out[share, 64:72, :] += jnp.dot(
            jnp.concatenate(sums, axis=0), gathered,
            preferred_element_type=F32, precision=lax.Precision.HIGHEST,
        )

    def second_half(q):
        add_taps(lax.rem(q + chunks - 1, chunks))
        earlier = jnp.maximum(q - 1, 0)
        taps = taps_of(earlier)
        lanes = chunk(q)
        share, at, own_groups = place(q)
        split_groups(
            split,
            (g_all[BLOCK:rows, lanes].astype(F32) * act_all[BLOCK:, lanes].astype(F32)).astype(BF16),
        )
        window = cot_all[BLOCK : 3 * BLOCK, lanes]
        for part in range(PARTS):
            for g in range(part * PER // PARTS, (part + 1) * PER // PARTS):
                own = slice(g * BLOCK, (g + 1) * BLOCK)
                ext = slice(g * EXT, (g + 1) * EXT)
                circ = circ_all[q, own, :]
                table[own, 0:LANES] = circ * win_mask[1, :, 0:LANES]
                table[own, LANES:] = circ * win_mask[1, :, LANES:]
                ext_table[ext, 0:LANES] = circ[0:EXT] * ext_mask[:, 0:LANES]
                ext_table[ext, LANES:] = circ[0:EXT] * ext_mask[:, LANES:]
            correlate(corr, split, cot_all, BLOCK, lanes, part)
            own = slice(part * PER // PARTS * BLOCK, (part + 1) * PER // PARTS * BLOCK)
            back_all[own, :] = jnp.dot(table[own, :], window, preferred_element_type=F32)
            short_back(earlier, taps, part)
        back_ext[...] = jnp.dot(
            ext_table[...], cot_all[2 * BLOCK : 4 * BLOCK, lanes], preferred_element_type=F32
        )
        short_terms(earlier)
        merge(merged, corr, diag_mask.at[1])
        ag_s[0:BLOCK, :] = ag_all[:, lanes].astype(F32)
        for part in range(PARTS):
            own = slice(BLOCK + part * SUB, BLOCK + (part + 1) * SUB)
            back = pick(back_all, part * SUB, SUB, BLOCK)
            ag_s[own, :] = (back * g_all[own, lanes].astype(F32)).astype(BF16).astype(F32)
            ggate_out[0, own, lanes] = (back * act_all[own, lanes].astype(F32)).astype(BF16)
        back = pick(back_ext, 0, EXT, EXT)
        ag_s[rows:, :] = (back * g_all[rows:, lanes].astype(F32)).astype(BF16).astype(F32)

    def one_piece(p, carry):
        piece(p).wait_recv()

        def inner(i, c):
            second_half(p * (chunks // PIECES) + i)
            return c

        return lax.fori_loop(0, chunks // PIECES, inner, carry)

    lax.fori_loop(0, PIECES, one_piece, 0)
    taps = taps_of(chunks - 1)
    for part in range(PARTS):
        short_back(chunks - 1, taps, part)
    short_terms(chunks - 1)
    add_taps(chunks - 1)
    for c in small:
        c.wait_send()
    gate_copy.wait_send()
    for p in range(PIECES):
        piece(p).wait_send()


def layer_pair(inputs, gates, cot, lengths, short_filter, long_filter):
    _, rows, channels = inputs.shape
    assert rows == 2 * BLOCK
    shares = lax.axis_size("fsdp")
    chunks = channels // LANES
    anyspace = pl.BlockSpec(memory_space=pl.ANY)
    vmem = pl.BlockSpec(memory_space=pltpu.VMEM)
    stack = PER * BLOCK
    return pl.pallas_call(
        pair_kernel,
        out_shape=(
            pltpu.VMEM(inputs.shape, BF16),
            pltpu.VMEM(inputs.shape, BF16),
            pltpu.VMEM((shares, PART, LANES), F32),
        ),
        in_specs=[pl.BlockSpec(memory_space=pltpu.SMEM), anyspace, anyspace, anyspace, vmem, vmem],
        out_specs=(vmem, vmem, vmem),
        scratch_shapes=[
            pltpu.VMEM((FILT, LANES), BF16),
            pltpu.VMEM((shares, FILT, LANES), BF16),
            pltpu.VMEM((shares, FILT, LANES), F32),
            pltpu.VMEM((rows, channels), BF16),
            pltpu.VMEM((16, channels), BF16),
            pltpu.VMEM((rows + EXT, channels), BF16),
            pltpu.VMEM((rows + 2 * BLOCK, channels), BF16),
            pltpu.VMEM((rows, channels), BF16),
            pltpu.VMEM((BLOCK, channels), BF16),
            pltpu.VMEM((chunks, stack, LANES), BF16),
            pltpu.VMEM((2, BLOCK, 2 * LANES), BF16),
            pltpu.VMEM((EXT, 2 * LANES), BF16),
            pltpu.VMEM((2, BLOCK, LANES), F32),
            pltpu.VMEM((SHORT - 1, rows, LANES), F32),
            pltpu.VMEM((SHORT - 1, rows, LANES), F32),
            pltpu.VMEM((rows + LANES, LANES), F32),
            pltpu.VMEM((rows + 8, LANES), F32),
            pltpu.VMEM((BLOCK, LANES), F32),
            pltpu.VMEM((BLOCK, LANES), F32),
            pltpu.VMEM((8 * SHORT, LANES), F32),
            pltpu.VMEM((PER * SUB, LANES), F32),
            pltpu.VMEM((rows + EXT, LANES), F32),
            pltpu.VMEM((stack, LANES), BF16),
            pltpu.VMEM((stack, 2 * LANES), BF16),
            pltpu.VMEM((PER * EXT, 2 * LANES), BF16),
            pltpu.VMEM((stack, 2 * LANES), F32),
            pltpu.VMEM((stack, LANES), F32),
            pltpu.VMEM((PER * EXT, LANES), F32),
            pltpu.SemaphoreType.DMA((3,)),
            pltpu.SemaphoreType.DMA((6,)),
            pltpu.SemaphoreType.DMA((6,)),
            pltpu.SemaphoreType.DMA((PIECES,)),
            pltpu.SemaphoreType.DMA((PIECES,)),
        ],
        compiler_params=pltpu.CompilerParams(
            collective_id=0, has_side_effects=True, vmem_limit_bytes=56 << 20
        ),
        name="layer_pair",
    )(lengths, inputs, gates, cot, short_filter, long_filter)


def reduce_kernel(scale, part, short_out, long_out, half, landed, bufs, cur, send_sem, recv_sem):
    side = 4
    f = lax.axis_index("fsdp")
    ctx = lax.axis_index("ctx")
    core, high = lax.rem(f, 2), f // 2
    y, low, x = lax.rem(ctx, side), lax.rem(ctx // side, side), ctx // (side * side)
    core_peer = (ctx, high * 2 + 1 - core)
    high_peer = (ctx, (1 - high) * 2 + core)
    axes = ((y, 1), (x, side * side), (low, side))

    def peer(axis, d):
        at, stride = axes[axis]
        return (ctx + (lax.rem(at + d, side) - at) * stride, f)

    barrier = pltpu.get_barrier_semaphore()
    for to in [core_peer, high_peer] + [peer(a, d) for a in range(3) for d in range(1, side)]:
        pl.semaphore_signal(barrier, inc=1, device_id=to, device_id_type=MESH)
    pl.semaphore_wait(barrier, 2 + 3 * (side - 1))

    swaps = [
        pltpu.make_async_remote_copy(
            part.at[2 * h + 1 - core], half.at[h], send_sem.at[0, h], recv_sem.at[0, h],
            device_id=core_peer, device_id_type=MESH,
        )
        for h in range(2)
    ]
    for c in swaps:
        c.start()
    for c in swaps:
        c.wait_recv()
    cur[0] = (part[2 * (1 - high) + core] + half[1 - high]).astype(BF16)
    cross = pltpu.make_async_remote_copy(
        cur.at[0], landed, send_sem.at[1, 0], recv_sem.at[1, 0],
        device_id=high_peer, device_id_type=MESH,
    )
    cross.start()
    total = part[2 * high + core] + half[high]
    cross.wait_recv()
    total = total + landed[...].astype(F32)
    sent = swaps + [cross]
    for axis in range(3):
        at = axes[axis][0]
        cur[axis + 1] = total.astype(BF16)
        copies = [
            pltpu.make_async_remote_copy(
                cur.at[axis + 1], bufs.at[axis, side - d],
                send_sem.at[axis + 2, d], recv_sem.at[axis + 2, side - d],
                device_id=peer(axis, d), device_id_type=MESH,
            )
            for d in range(1, side)
        ]
        for c in copies:
            c.start()
        sent += copies
        bufs[axis, 0] = cur[axis + 1]
        for c in copies:
            c.wait_recv()
        total = jnp.zeros(total.shape, F32)
        for place in range(side):
            total = total + bufs[axis, lax.rem(place - at + side, side)].astype(F32)
    total = total * scale
    long_out[...] = total[0:64]
    short_out[...] = total[64 : 64 + SHORT, 0:64]
    for c in sent:
        c.wait_send()


def reduce(part, scale, short_shape, long_shape):
    vmem = pl.BlockSpec(memory_space=pltpu.VMEM)
    return pl.pallas_call(
        functools.partial(reduce_kernel, scale),
        out_shape=(
            jax.ShapeDtypeStruct(short_shape, F32),
            jax.ShapeDtypeStruct(long_shape, F32),
        ),
        in_specs=[vmem],
        out_specs=(vmem, vmem),
        scratch_shapes=[
            pltpu.VMEM((2, PART, LANES), F32),
            pltpu.VMEM((PART, LANES), BF16),
            pltpu.VMEM((3, 4, PART, LANES), BF16),
            pltpu.VMEM((4, PART, LANES), BF16),
            pltpu.SemaphoreType.DMA((5, 4)),
            pltpu.SemaphoreType.DMA((5, 4)),
        ],
        compiler_params=pltpu.CompilerParams(
            collective_id=1, has_side_effects=True, vmem_limit_bytes=4 << 20
        ),
        name="sum_terms",
    )(part)


def on_device(inputs, gates, grad_out, doc_lengths, short_filter, long_filter):
    rows = inputs.shape[1]
    grad_inputs, grad_gates, part = layer_pair(
        inputs, gates, grad_out, doc_lengths, short_filter, jnp.transpose(long_filter)
    )
    scale = 1.0 / math.sqrt(lax.axis_size("fsdp") * lax.axis_size("ctx") * rows)
    short_share, long_share = reduce(part, scale, short_filter.shape, long_filter.shape[::-1])
    return grad_inputs, grad_gates, short_share, jnp.transpose(long_share)


def solution(mesh):
    rows = P("fsdp", "ctx", None)
    return jax.shard_map(
        on_device,
        mesh=mesh,
        in_specs=(rows, rows, rows, P("fsdp", None), P(None, "fsdp"), P(None, "fsdp")),
        out_specs=(rows, rows, P(None, "fsdp"), P(None, "fsdp")),
        check_vma=False,
    )
```

```python
import functools
import math

import jax
import jax.numpy as jnp
from jax import lax
from jax.experimental import pallas as pl
from jax.experimental.pallas import tpu as pltpu
from jax.sharding import PartitionSpec as P

MESH = pl.DeviceIdType.MESH
F32 = jnp.float32
BF16 = jnp.bfloat16

LANES = 128
TAPS = 128
SHORT = 7
BLOCK = 128
SUB = 32
HALO = 144
EXT = 16
WIDTH = 16
PER = LANES // WIDTH
PARTS = 4
PIECES = 8
FILT = 80
PART = 80


def ring(axis, distance):
    n = lax.axis_size(axis)
    return lax.rem(lax.axis_index(axis) + distance + n, n)


def prepare(lengths, win_mask, ext_mask, diag_mask, fwd_mask, bwd_mask, rcol, row0):
    docs = lengths.shape[1]
    rows = fwd_mask.shape[1]
    lane_pos = row0 + lax.broadcasted_iota(jnp.int32, (8, 512), 1)

    def one_doc(d, carry):
        end, start = carry
        end = end + lengths[0, d]
        return end, jnp.where(lane_pos >= end, end, start)

    _, start = lax.fori_loop(0, docs, one_doc, (jnp.int32(0), jnp.zeros((8, 512), jnp.int32)))
    passed = (lane_pos - start).astype(F32)
    for k in range(3):
        own = slice(k * LANES, (k + 1) * LANES)
        turned = jnp.transpose(jnp.broadcast_to(passed[0:1, own], (LANES, LANES)))
        rcol[k * LANES : k * LANES + LANES, :] = turned
    for j in range(1, SHORT):
        fwd_mask[j - 1] = (rcol[0:rows, :] >= j).astype(F32)
        bwd_mask[j - 1] = (rcol[j : j + rows, :] >= j).astype(F32)
    s_rel = lax.broadcasted_iota(jnp.int32, (BLOCK, LANES), 0)
    lane = lax.broadcasted_iota(jnp.int32, (BLOCK, LANES), 1)

    def starts_at(first, count):
        return jnp.broadcast_to(start[0:1, first : first + LANES], (count, LANES))

    for b in range(rows // BLOCK):
        s_abs = row0 + b * BLOCK + s_rel
        near = lane >= s_rel
        first = b * BLOCK
        m0 = jnp.where(near & (starts_at(first, BLOCK) <= s_abs), 1.0, 0.0)
        m1 = jnp.where(near | (starts_at(first + LANES, BLOCK) > s_abs), 0.0, 1.0)
        win_mask[b, :, 0:LANES] = m0.astype(BF16)
        win_mask[b, :, LANES:] = m1.astype(BF16)
        for k in range(BLOCK // SUB):
            own = slice(k * SUB, (k + 1) * SUB)
            first = b * BLOCK + k * SUB
            near = lane[0:SUB] >= s_rel[0:SUB]
            target = jnp.where(near, starts_at(first, SUB), starts_at(first + LANES, SUB))
            diag_mask[b, own, :] = jnp.where(target <= s_abs[own], 1.0, 0.0)
    s_abs = row0 + rows + s_rel[0:EXT]
    near = (lane >= s_rel)[0:EXT]
    m0 = jnp.where(near & (starts_at(rows, EXT) <= s_abs), 1.0, 0.0)
    m1 = jnp.where(near | (starts_at(rows + LANES, EXT) > s_abs), 0.0, 1.0)
    ext_mask[:, 0:LANES] = m0.astype(BF16)
    ext_mask[:, LANES:] = m1.astype(BF16)


def chunk(q):
    return pl.ds(pl.multiple_of(q * LANES, LANES), LANES)


def lane_groups(rows):
    return lax.broadcasted_iota(jnp.int32, (rows, LANES), 1) // WIDTH


def chunk_taps(filt32, share, at):
    spread = (
        lax.broadcasted_iota(jnp.int32, (LANES, LANES), 0)
        == at * PER + lax.broadcasted_iota(jnp.int32, (LANES, LANES), 1) // WIDTH
    ).astype(F32)
    return jnp.dot(
        filt32[share, 64:72, :].astype(BF16), spread.astype(BF16), preferred_element_type=F32
    )


def pick(stacked, first, count, stride):
    group = lane_groups(count)
    picked = stacked[first : first + count, :]
    for g in range(1, PER):
        at = g * stride + first
        picked = jnp.where(group == g, stacked[at : at + count, :], picked)
    return picked


def split_groups(split, gated):
    group = lane_groups(SUB)
    for k in range(BLOCK // SUB):
        for g in range(PER):
            at = (k * PER + g) * SUB
            split[at : at + SUB, :] = jnp.where(
                group == g, gated[k * SUB : (k + 1) * SUB, :], jnp.zeros((), BF16)
            )


def correlate(corr, split, cot_all, first, lanes, k):
    own = slice(k * PER * SUB, (k + 1) * PER * SUB)
    reach = SUB + TAPS
    window = cot_all[first + k * SUB : first + k * SUB + reach, lanes]
    corr[own, 0:reach] = lax.dot_general(
        split[own, :], window, (((1,), (1,)), ((), ())), preferred_element_type=F32
    )


def merge(merged, corr, diag):
    lane8 = lax.broadcasted_iota(jnp.int32, (8, LANES), 1)
    row8 = lax.broadcasted_iota(jnp.int32, (8, LANES), 0)
    for g in range(PER):
        for i in range(SUB // 8):
            total = jnp.zeros((8, LANES), F32)
            for k in range(BLOCK // SUB):
                at_row = (k * PER + g) * SUB + 8 * i
                total = total + diag[k * SUB + 8 * i : k * SUB + 8 * i + 8, :] * jnp.where(
                    lane8 >= row8 + 8 * i,
                    corr[at_row : at_row + 8, 0:LANES],
                    corr[at_row : at_row + 8, LANES:],
                )
            merged[g * SUB + 8 * i : g * SUB + 8 * i + 8, :] = total


def line_up(merged):
    row8 = lax.broadcasted_iota(jnp.int32, (8, LANES), 0)
    tap_rows = []
    for g in range(PER):
        total = merged[g * SUB : g * SUB + 8, :]
        for i in range(1, SUB // 8):
            at = g * SUB + 8 * i
            total = total + pltpu.roll(merged[at : at + 8, :], LANES - 8 * i, 1)
        for bit in (1, 2, 4):
            total = jnp.where((row8 & bit) > 0, pltpu.roll(total, LANES - bit, 1), total)
        tap_rows.append(jnp.sum(total, axis=0, keepdims=True))
    return jnp.concatenate(tap_rows, axis=0)


def pair_kernel(
    lengths, inputs, gates, cot, short_ref, long_ref,
    gin_out, ggate_out, part_out,
    mine, filt, filt32, x_all, before_all, g_all, cot_all, act_all, ag_all, circ_all,
    win_mask, ext_mask, diag_mask, fwd_mask, bwd_mask, rcol,
    x_s, act_next, act_s, terms, merged, ag_s, split, table, ext_table, corr, back_all, back_ext,
    own_sem, send_sem, recv_sem, cot_send, cot_recv,
):
    rows, channels = inputs.shape[1:]
    chunks = channels // LANES
    per_share = 64 // PER
    width = channels // PIECES
    peers = lax.axis_size("fsdp")
    f = lax.axis_index("fsdp")
    ctx = lax.axis_index("ctx")
    row0 = ctx * rows
    after, before = ring("ctx", 1), ring("ctx", -1)
    barrier = pltpu.get_barrier_semaphore()
    for to in (after, before):
        pl.semaphore_signal(barrier, inc=1, device_id=(to, f), device_id_type=MESH)
    for d in range(1, peers):
        pl.semaphore_signal(barrier, inc=1, device_id=(ctx, ring("fsdp", d)), device_id_type=MESH)
    local = [
        pltpu.make_async_copy(inputs.at[0], x_all, own_sem.at[0]),
        pltpu.make_async_copy(gates.at[0], g_all.at[pl.ds(0, rows), :], own_sem.at[1]),
        pltpu.make_async_copy(cot.at[0], cot_all.at[pl.ds(0, rows), :], own_sem.at[2]),
    ]
    for c in local:
        c.start()
    mine[...] = jnp.zeros_like(mine)
    mine[0:64, :] = long_ref[...]
    mine[64 : 64 + SHORT, 0:64] = short_ref[...]
    pl.semaphore_wait(barrier, peers + 1)
    small = []
    for d in range(1, peers):
        small.append(
            pltpu.make_async_remote_copy(
                mine, filt.at[f], send_sem.at[d], recv_sem.at[d],
                device_id=(ctx, ring("fsdp", d)), device_id_type=MESH,
            )
        )
    small.append(
        pltpu.make_async_remote_copy(
            inputs.at[0, pl.ds(rows - 16, 16), :], before_all, send_sem.at[4], recv_sem.at[4],
            device_id=(after, f), device_id_type=MESH,
        )
    )
    for c in small:
        c.start()

    def piece(p):
        lanes = pl.ds(pl.multiple_of(p * width, LANES), width)
        return pltpu.make_async_remote_copy(
            cot.at[0, pl.ds(0, HALO), lanes], cot_all.at[pl.ds(rows, HALO), lanes],
            cot_send.at[p], cot_recv.at[p],
            device_id=(before, f), device_id_type=MESH,
        )

    gate_copy = pltpu.make_async_remote_copy(
        gates.at[0, pl.ds(0, EXT), :], g_all.at[pl.ds(rows, EXT), :],
        send_sem.at[5], recv_sem.at[5],
        device_id=(before, f), device_id_type=MESH,
    )
    gate_copy.start()
    for p in range(PIECES):
        piece(lax.rem(f * (PIECES // peers) + p, PIECES)).start()

    prepare(lengths, win_mask, ext_mask, diag_mask, fwd_mask, bwd_mask, rcol, row0)
    cot_all[rows + HALO :, :] = jnp.zeros((cot_all.shape[0] - rows - HALO, channels), BF16)
    part_out[...] = jnp.zeros_like(part_out)
    filt32[f] = mine[...].astype(F32)
    small[-1].wait_recv()
    for c in local:
        c.wait()
    origin = f * per_share

    def place(q):
        share, at = q // per_share, lax.rem(q, per_share)
        return share, at, pl.ds(pl.multiple_of(at * PER, PER), PER)

    def load_next(q):
        lanes = chunk(q)
        x_s[0:8, :] = before_all[:, lanes].astype(F32)[8:16]
        x_s[8:, :] = x_all[:, lanes].astype(F32)

    def forward(q, taps, part):
        lanes = chunk(q)
        size = rows // PARTS
        own = slice(part * size, (part + 1) * size)
        act = taps[0:1, :] * x_s[8 + part * size : 8 + (part + 1) * size, :]
        for j in range(1, SHORT):
            at = 8 - j + part * size
            act = act + fwd_mask[j - 1, own, :] * (taps[j : j + 1, :] * x_s[at : at + size, :])
        act = act.astype(BF16)
        act_all[own, lanes] = act
        if (part + 1) * size <= BLOCK:
            act_next[own, :] = act.astype(F32)

    def taps_of(q):
        share, at, _ = place(q)
        return chunk_taps(filt32, share, at)

    def add_taps(q):
        share, _, own_groups = place(q)
        part_out[share, own_groups, :] += line_up(merged)

    merged[...] = jnp.zeros_like(merged)
    load_next(origin)
    for part in range(PARTS):
        forward(origin, taps_of(origin), part)

    def first_half(step, carry):
        q = lax.rem(origin + step, chunks)
        lanes = chunk(q)
        share, at, own_groups = place(q)
        long_rows = filt32[share, own_groups, :]
        add_taps(lax.rem(q + chunks - 1, chunks))
        gate = g_all[0:BLOCK, lanes].astype(F32)
        act = act_next[...]
        act_s[...] = act
        split_groups(split, (gate * act).astype(BF16))
        later = lax.rem(q + 1, chunks)
        taps = taps_of(later)
        load_next(later)
        window = cot_all[0 : 2 * BLOCK, lanes]
        for part in range(PARTS):
            for g in range(part * PER // PARTS, (part + 1) * PER // PARTS):
                own = slice(g * BLOCK, (g + 1) * BLOCK)
                circ = pltpu.roll(
                    jnp.broadcast_to(long_rows[g : g + 1, :], (BLOCK, LANES)), 0, 1,
                    stride=1, stride_axis=0,
                ).astype(BF16)
                circ_all[q, own, :] = circ
                table[own, 0:LANES] = circ * win_mask[0, :, 0:LANES]
                table[own, LANES:] = circ * win_mask[0, :, LANES:]
            correlate(corr, split, cot_all, 0, lanes, part)
            own = slice(part * PER // PARTS * BLOCK, (part + 1) * PER // PARTS * BLOCK)
            back_all[own, :] = jnp.dot(table[own, :], window, preferred_element_type=F32)
            forward(later, taps, part)
        merge(merged, corr, diag_mask.at[0])
        for part in range(PARTS):
            own = slice(part * SUB, (part + 1) * SUB)
            back = pick(back_all, part * SUB, SUB, BLOCK)
            ag_all[own, lanes] = (back * g_all[own, lanes].astype(F32)).astype(BF16)
            ggate_out[0, own, lanes] = (back * act_s[own, :]).astype(BF16)
        return carry

    lax.fori_loop(0, per_share - 1, first_half, 0)
    for d in range(1, peers):
        small[d - 1].wait_recv()
    for d in range(1, peers):
        share = ring("fsdp", d)
        filt32[share] = filt[share].astype(F32)
    lax.fori_loop(per_share - 1, chunks, first_half, 0)
    gate_copy.wait_recv()

    ag_s[...] = jnp.zeros_like(ag_s)

    def short_back(q, taps, part):
        lanes = chunk(q)
        size = rows // PARTS
        first = part * size
        own = slice(first, first + size)
        x = x_all[own, lanes].astype(F32)
        gin = jnp.zeros((size, LANES), F32)
        for j in range(SHORT):
            moved = ag_s[first + j : first + j + size, :]
            if j:
                moved = bwd_mask[j - 1, own, :] * moved
            gin = gin + taps[j : j + 1, :] * moved
            product = jnp.sum((moved * x).reshape(size // 8, 8, LANES), axis=0)
            if part:
                product = product + terms[8 * j : 8 * j + 8, :]
            terms[8 * j : 8 * j + 8, :] = product
        gin_out[0, own, lanes] = gin.astype(BF16)

    def short_terms(q):
        share, at, _ = place(q)
        sums = [
            jnp.sum(terms[8 * j : 8 * j + 8, :], axis=0, keepdims=True) for j in range(SHORT)
        ] + [jnp.zeros((1, LANES), F32)]
        gathered = (
            lax.broadcasted_iota(jnp.int32, (LANES, LANES), 1)
            == at * PER + lax.broadcasted_iota(jnp.int32, (LANES, LANES), 0) // WIDTH
        ).astype(F32)
        part_out[share, 64:72, :] += jnp.dot(
            jnp.concatenate(sums, axis=0), gathered,
            preferred_element_type=F32, precision=lax.Precision.HIGHEST,
        )

    def second_half(q):
        add_taps(lax.rem(q + chunks - 1, chunks))
        earlier = lax.rem(q + chunks - 1, chunks)
        taps = taps_of(earlier)
        lanes = chunk(q)
        share, at, own_groups = place(q)
        split_groups(
            split,
            (g_all[BLOCK:rows, lanes].astype(F32) * act_all[BLOCK:, lanes].astype(F32)).astype(BF16),
        )
        window = cot_all[BLOCK : 3 * BLOCK, lanes]
        for part in range(PARTS):
            for g in range(part * PER // PARTS, (part + 1) * PER // PARTS):
                own = slice(g * BLOCK, (g + 1) * BLOCK)
                ext = slice(g * EXT, (g + 1) * EXT)
                circ = circ_all[q, own, :]
                table[own, 0:LANES] = circ * win_mask[1, :, 0:LANES]
                table[own, LANES:] = circ * win_mask[1, :, LANES:]
                ext_table[ext, 0:LANES] = circ[0:EXT] * ext_mask[:, 0:LANES]
                ext_table[ext, LANES:] = circ[0:EXT] * ext_mask[:, LANES:]
            correlate(corr, split, cot_all, BLOCK, lanes, part)
            own = slice(part * PER // PARTS * BLOCK, (part + 1) * PER // PARTS * BLOCK)
            back_all[own, :] = jnp.dot(table[own, :], window, preferred_element_type=F32)
            short_back(earlier, taps, part)
        back_ext[...] = jnp.dot(
            ext_table[...], cot_all[2 * BLOCK : 4 * BLOCK, lanes], preferred_element_type=F32
        )
        short_terms(earlier)
        merge(merged, corr, diag_mask.at[1])
        ag_s[0:BLOCK, :] = ag_all[:, lanes].astype(F32)
        for part in range(PARTS):
            own = slice(BLOCK + part * SUB, BLOCK + (part + 1) * SUB)
            back = pick(back_all, part * SUB, SUB, BLOCK)
            ag_s[own, :] = (back * g_all[own, lanes].astype(F32)).astype(BF16).astype(F32)
            ggate_out[0, own, lanes] = (back * act_all[own, lanes].astype(F32)).astype(BF16)
        back = pick(back_ext, 0, EXT, EXT)
        ag_s[rows:, :] = (back * g_all[rows:, lanes].astype(F32)).astype(BF16).astype(F32)

    def one_piece(step, carry):
        p = lax.rem(f * (PIECES // peers) + step, PIECES)
        piece(p).wait_recv()

        def inner(i, c):
            second_half(p * (chunks // PIECES) + i)
            return c

        return lax.fori_loop(0, chunks // PIECES, inner, carry)

    lax.fori_loop(0, PIECES, one_piece, 0)
    last = lax.rem(origin + chunks - 1, chunks)
    taps = taps_of(last)
    for part in range(PARTS):
        short_back(last, taps, part)
    short_terms(last)
    add_taps(last)
    for c in small:
        c.wait_send()
    gate_copy.wait_send()
    for p in range(PIECES):
        piece(p).wait_send()


def layer_pair(inputs, gates, cot, lengths, short_filter, long_filter):
    _, rows, channels = inputs.shape
    assert rows == 2 * BLOCK
    shares = lax.axis_size("fsdp")
    chunks = channels // LANES
    anyspace = pl.BlockSpec(memory_space=pl.ANY)
    vmem = pl.BlockSpec(memory_space=pltpu.VMEM)
    stack = PER * BLOCK
    return pl.pallas_call(
        pair_kernel,
        out_shape=(
            pltpu.VMEM(inputs.shape, BF16),
            pltpu.VMEM(inputs.shape, BF16),
            pltpu.VMEM((shares, PART, LANES), F32),
        ),
        in_specs=[pl.BlockSpec(memory_space=pltpu.SMEM), anyspace, anyspace, anyspace, vmem, vmem],
        out_specs=(vmem, vmem, vmem),
        scratch_shapes=[
            pltpu.VMEM((FILT, LANES), BF16),
            pltpu.VMEM((shares, FILT, LANES), BF16),
            pltpu.VMEM((shares, FILT, LANES), F32),
            pltpu.VMEM((rows, channels), BF16),
            pltpu.VMEM((16, channels), BF16),
            pltpu.VMEM((rows + EXT, channels), BF16),
            pltpu.VMEM((rows + 2 * BLOCK, channels), BF16),
            pltpu.VMEM((rows, channels), BF16),
            pltpu.VMEM((BLOCK, channels), BF16),
            pltpu.VMEM((chunks, stack, LANES), BF16),
            pltpu.VMEM((2, BLOCK, 2 * LANES), BF16),
            pltpu.VMEM((EXT, 2 * LANES), BF16),
            pltpu.VMEM((2, BLOCK, LANES), F32),
            pltpu.VMEM((SHORT - 1, rows, LANES), F32),
            pltpu.VMEM((SHORT - 1, rows, LANES), F32),
            pltpu.VMEM((rows + LANES, LANES), F32),
            pltpu.VMEM((rows + 8, LANES), F32),
            pltpu.VMEM((BLOCK, LANES), F32),
            pltpu.VMEM((BLOCK, LANES), F32),
            pltpu.VMEM((8 * SHORT, LANES), F32),
            pltpu.VMEM((PER * SUB, LANES), F32),
            pltpu.VMEM((rows + EXT, LANES), F32),
            pltpu.VMEM((stack, LANES), BF16),
            pltpu.VMEM((stack, 2 * LANES), BF16),
            pltpu.VMEM((PER * EXT, 2 * LANES), BF16),
            pltpu.VMEM((stack, 2 * LANES), F32),
            pltpu.VMEM((stack, LANES), F32),
            pltpu.VMEM((PER * EXT, LANES), F32),
            pltpu.SemaphoreType.DMA((3,)),
            pltpu.SemaphoreType.DMA((6,)),
            pltpu.SemaphoreType.DMA((6,)),
            pltpu.SemaphoreType.DMA((PIECES,)),
            pltpu.SemaphoreType.DMA((PIECES,)),
        ],
        compiler_params=pltpu.CompilerParams(
            collective_id=0, has_side_effects=True, vmem_limit_bytes=56 << 20
        ),
        name="layer_pair",
    )(lengths, inputs, gates, cot, short_filter, long_filter)


def reduce_kernel(scale, part, short_out, long_out, half, landed, bufs, cur, send_sem, recv_sem):
    side = 4
    f = lax.axis_index("fsdp")
    ctx = lax.axis_index("ctx")
    core, high = lax.rem(f, 2), f // 2
    y, low, x = lax.rem(ctx, side), lax.rem(ctx // side, side), ctx // (side * side)
    core_peer = (ctx, high * 2 + 1 - core)
    high_peer = (ctx, (1 - high) * 2 + core)
    axes = ((y, 1), (x, side * side), (low, side))

    def peer(axis, d):
        at, stride = axes[axis]
        return (ctx + (lax.rem(at + d, side) - at) * stride, f)

    barrier = pltpu.get_barrier_semaphore()
    for to in [core_peer, high_peer] + [peer(a, d) for a in range(3) for d in range(1, side)]:
        pl.semaphore_signal(barrier, inc=1, device_id=to, device_id_type=MESH)
    pl.semaphore_wait(barrier, 2 + 3 * (side - 1))

    swaps = [
        pltpu.make_async_remote_copy(
            part.at[2 * h + 1 - core], half.at[h], send_sem.at[0, h], recv_sem.at[0, h],
            device_id=core_peer, device_id_type=MESH,
        )
        for h in range(2)
    ]
    for c in swaps:
        c.start()
    for c in swaps:
        c.wait_recv()
    cur[0] = (part[2 * (1 - high) + core] + half[1 - high]).astype(BF16)
    cross = pltpu.make_async_remote_copy(
        cur.at[0], landed, send_sem.at[1, 0], recv_sem.at[1, 0],
        device_id=high_peer, device_id_type=MESH,
    )
    cross.start()
    total = part[2 * high + core] + half[high]
    cross.wait_recv()
    total = total + landed[...].astype(F32)
    sent = swaps + [cross]
    for axis in range(3):
        at = axes[axis][0]
        cur[axis + 1] = total.astype(BF16)
        copies = [
            pltpu.make_async_remote_copy(
                cur.at[axis + 1], bufs.at[axis, side - d],
                send_sem.at[axis + 2, d], recv_sem.at[axis + 2, side - d],
                device_id=peer(axis, d), device_id_type=MESH,
            )
            for d in range(1, side)
        ]
        for c in copies:
            c.start()
        sent += copies
        bufs[axis, 0] = cur[axis + 1]
        for c in copies:
            c.wait_recv()
        total = jnp.zeros(total.shape, F32)
        for place in range(side):
            total = total + bufs[axis, lax.rem(place - at + side, side)].astype(F32)
    total = total * scale
    long_out[...] = total[0:64]
    short_out[...] = total[64 : 64 + SHORT, 0:64]
    for c in sent:
        c.wait_send()


def reduce(part, scale, short_shape, long_shape):
    vmem = pl.BlockSpec(memory_space=pltpu.VMEM)
    return pl.pallas_call(
        functools.partial(reduce_kernel, scale),
        out_shape=(
            jax.ShapeDtypeStruct(short_shape, F32),
            jax.ShapeDtypeStruct(long_shape, F32),
        ),
        in_specs=[vmem],
        out_specs=(vmem, vmem),
        scratch_shapes=[
            pltpu.VMEM((2, PART, LANES), F32),
            pltpu.VMEM((PART, LANES), BF16),
            pltpu.VMEM((3, 4, PART, LANES), BF16),
            pltpu.VMEM((4, PART, LANES), BF16),
            pltpu.SemaphoreType.DMA((5, 4)),
            pltpu.SemaphoreType.DMA((5, 4)),
        ],
        compiler_params=pltpu.CompilerParams(
            collective_id=1, has_side_effects=True, vmem_limit_bytes=4 << 20
        ),
        name="sum_terms",
    )(part)


def on_device(inputs, gates, grad_out, doc_lengths, short_filter, long_filter):
    rows = inputs.shape[1]
    grad_inputs, grad_gates, part = layer_pair(
        inputs, gates, grad_out, doc_lengths, short_filter, jnp.transpose(long_filter)
    )
    scale = 1.0 / math.sqrt(lax.axis_size("fsdp") * lax.axis_size("ctx") * rows)
    short_share, long_share = reduce(part, scale, short_filter.shape, long_filter.shape[::-1])
    return grad_inputs, grad_gates, short_share, jnp.transpose(long_share)


def solution(mesh):
    rows = P("fsdp", "ctx", None)
    return jax.shard_map(
        on_device,
        mesh=mesh,
        in_specs=(rows, rows, rows, P("fsdp", None), P(None, "fsdp"), P(None, "fsdp")),
        out_specs=(rows, rows, P(None, "fsdp"), P(None, "fsdp")),
        check_vma=False,
    )
```
